128 devices in a mesh: pool: 2 (over core), grp: 8 (over x, z_lo), shard: 8 (over y, z_hi).
Axes of the slice: x: 4, y: 4, z: 4 (z_hi: 2, z_lo: 2; z = z_hi * 2 + z_lo), core: 2. Of those that a mesh axis runs over, the one named last changes fastest.
Arguments:
- queries: bfloat16 [1024, 6144], P(('grp', 'shard'), 'pool')
- new_keys: bfloat16 [1024, 1024], P(('grp', 'shard'), 'pool'), may hold values from -6 to 6
- new_values: bfloat16 [1024, 1024], P(('grp', 'shard'), 'pool'), may hold values from -6 to 6
- fork_map: int32 [1024], P(('grp', 'shard')), may hold values from 0 to 127, as said below
- key_cache: bfloat16 [128, 1024, 1024], P(('grp', 'shard'), None, 'pool')
- value_cache: bfloat16 [128, 1024, 1024], P(('grp', 'shard'), None, 'pool'), may hold values from -6 to 6
- cache_lengths: int32 [128], P(('grp', 'shard')), may hold values from 256 to 1024
- residual: bfloat16 [1024, 6144], P(('grp', 'shard')), may hold values from -1.75 to 1.75
- norm_gain: bfloat16 [6144], replicated, may hold values from 0.5 to 1.5
- expert_ids: int32 [1024, 2], P(('grp', 'shard')), may hold values from 0 to 7, all different within a row; in each aligned block of 16 rows (0 to 15, 16 to 31, ...) at most 8 rows name the same one
- gate_weights: float32 [1024, 2], P(('grp', 'shard')), may hold values from 0.1 to 1
- w_gate: bfloat16 [8, 6144, 8192], P('grp', None, ('pool', 'shard')), may hold values from -0.078125 to 0.078125
- w_up: bfloat16 [8, 6144, 8192], P('grp', None, ('pool', 'shard')), may hold values from -0.078125 to 0.078125
- w_down: bfloat16 [8, 8192, 6144], P('grp', ('pool', 'shard')), may hold values from -0.0625 to 0.0625
Outputs:
- layer_out: bfloat16 [1024, 6144], P(('grp', 'shard'))
The draws below stay inside these ranges and needn't reach their ends.
Inputs may be any that keep to these rules, and one draw needn't show every extreme that they name: Row r forks a prompt held beside it: fork_map[r] // 2 == r // 16. `expert_ids`: each row names 2 different experts; among the 16 rows of one device no expert is named more than 8 times.
All inputs are finite; a program needn't handle non-finite values.
Results may differ from the reference program's by a relative error of at most 0.02.
Values may be sent and summed in bfloat16 or wider, within the bound.
A program may use at most 128 MiB of HBM per device.

```python
import math
import jax
import jax.numpy as jnp
import numpy as np
from jax import lax

D = 6144
QH = 48
KVH = 8
HD = 128
FF = 8192
TOP = 2
ROW_DEV = 16
PROMPT_DEV = 2
CACHE = 1024
CAP = 8
EXPERTS = 8
ROWS = 1024
PROMPTS = 128


def cache_keys(key):
    return jax.random.normal(jax.random.fold_in(key, 11), (PROMPTS, CACHE, KVH * HD), jnp.float32)


def prompt_rows(key):
    offsets = jax.random.randint(jax.random.fold_in(key, 12), (ROWS,), 0, PROMPT_DEV)
    return (jnp.arange(ROWS, dtype=jnp.int32) // ROW_DEV * PROMPT_DEV + offsets).astype(jnp.int32)


def draw_key_cache(key, part):
    return cache_keys(key).astype(jnp.bfloat16)


def draw_fork_map(key, part):
    return prompt_rows(key)


def draw_cache_lengths(key, part):
    key = jax.random.fold_in(key, 2)
    lengths = jax.random.randint(jax.random.fold_in(key, 1), (PROMPTS,), CACHE // 4, CACHE + 1)
    place = jax.random.randint(jax.random.fold_in(key, 2), (), 0, PROMPTS)
    return jnp.where(jnp.arange(PROMPTS, dtype=jnp.int32) == place, CACHE, lengths).astype(jnp.int32)


def draw_queries(key, part):
    key = jax.random.fold_in(key, 3)
    values = 1.5 * jax.random.normal(jax.random.fold_in(key, 1), (ROWS, QH * HD), jnp.float32)
    return values.astype(jnp.bfloat16)


def shard_levels(own_key, shape, split, smallest, top_value):
    gain = 1.0
    for dim, parts in split:
        steps = jax.random.uniform(jax.random.fold_in(jax.random.fold_in(own_key, 6), dim), (parts,), jnp.float32, smallest / len(split), top_value / len(split))
        gain = gain * jnp.repeat(jnp.exp(steps), shape[dim] // parts).reshape((-1,) + (1,) * (len(shape) - 1 - dim))
    return gain


def assign_block(own_key, own, number, rows, number_of, top, most, slope):
    ranking = jax.random.permutation(own_key, number_of)
    packed, usual = shares(number_of, rows * top, most, slope, True), shares(number_of, rows * top, most, slope, False)
    places = jnp.arange(number_of)

    def named(sizes, rotation):
        used = int((sizes > 0).sum())
        fixed = max(1, used // 4)
        moved = fixed + (places - fixed + rotation * (used - fixed)) % max(1, number_of - fixed)
        return jnp.zeros((number_of,), jnp.int32).at[ranking[jnp.where(places < fixed, places, moved)]].set(jnp.asarray(sizes, jnp.int32))

    sizes = jnp.where(number % 4 == 0, named(packed, number // 4), named(usual, number - number // 4 - 1))
    mixed = jax.random.permutation(jax.random.fold_in(own, 3), number_of)
    source_of, taker = mixed[0:number_of // 2 * 2:2], mixed[1:number_of // 2 * 2:2]
    room = jnp.minimum(sizes[source_of] - 1, most - sizes[taker]) // 2
    room = jnp.where((source_of == ranking[0]) | (taker == ranking[0]) | (sizes[taker] == 0), 0, jnp.maximum(room, 0))
    moved = jax.random.randint(jax.random.fold_in(own, 4), (number_of // 2,), 0, 1 << 20) % (room + 1)
    sizes = sizes.at[source_of].add(-moved).at[taker].add(moved)
    items = jnp.searchsorted(jnp.cumsum(sizes), jnp.arange(rows * top), side="right").astype(jnp.int32)
    table = items.reshape(top, rows).T
    table = table[jax.random.permutation(jax.random.fold_in(own, 1), rows)]
    rotation = jax.random.randint(jax.random.fold_in(own, 2), (rows, 1), 0, top)
    return jnp.take_along_axis(table, (jnp.arange(top)[None, :] + rotation) % top, axis=1)


def shares(number_of, total, most, slope, full):
    loads = [(1 << 20) // math.isqrt(rank ** slope) + 1 for rank in range(1, number_of + 1)]
    largest = most if full else min(most, max(-(-total // number_of), total * loads[0] // sum(loads)))
    least = 1 if total - largest >= number_of - 1 else 0
    given, spare = [largest] + [least] * (number_of - 1), total - largest - least * (number_of - 1)
    while spare > 0:
        free = [i for i in range(1, number_of) if given[i] < largest] or [i for i in range(1, number_of) if given[i] < most]
        pool, budget = sum([loads[i] for i in free]), spare
        for i in free:
            extra = min(most - given[i], max(1, budget * loads[i] // pool), spare)
            given[i] = given[i] + extra
            spare = spare - extra
    return np.array(given)


def centred(stream_key, dims, spread, most, cuts=(), kind=jnp.bfloat16):
    level = shard_levels(stream_key, dims, cuts, -0.22, 0.18) if cuts else 1.0
    values = jax.random.normal(stream_key, dims, jnp.float32) * spread * level
    return jnp.minimum(jnp.maximum(values, -most), most).astype(kind)


def setup_inputs(seed: int = 0) -> dict:
    splits = jax.random.split(jax.random.key(seed), 15)
    queries = draw_queries(jax.random.fold_in(splits[14], 71), 0)
    new_keys = centred(splits[1], (ROWS, KVH * HD), 1.0, 6.0, ((0, 64), (1, 2)))
    new_values = centred(splits[2], (ROWS, KVH * HD), 1.0, 6.0, ((0, 64), (1, 2)))
    fork_map = draw_fork_map(jax.random.fold_in(splits[14], 71), 0)
    key_cache = draw_key_cache(jax.random.fold_in(splits[14], 71), 0)
    value_cache = centred(splits[5], (PROMPTS, CACHE, KVH * HD), 1.0, 6.0, ((0, 64), (2, 2)))
    cache_lengths = draw_cache_lengths(jax.random.fold_in(splits[14], 71), 0)
    residual = centred(splits[7], (ROWS, D), 0.3, 1.75, ((0, 64),))
    norm_gain = jnp.clip(1.0 + 0.1 * jax.random.normal(splits[8], (D,), jnp.float32), 0.5, 1.5).astype(jnp.bfloat16)
    expert_ids_keys = jax.random.split(jax.random.fold_in(splits[9], 1), ROWS // ROW_DEV)
    expert_ids_turns = jax.random.permutation(jax.random.fold_in(splits[9], 3), ROWS // ROW_DEV)
    expert_ids = jax.vmap(lambda own, number: assign_block(jax.random.fold_in(splits[9], 2), own, number, ROW_DEV, EXPERTS, TOP, CAP, 2))(expert_ids_keys, expert_ids_turns).reshape((ROWS, TOP))
    gate_weights = jnp.clip(jnp.exp(math.log(1.0) - 2.3025851 * jax.random.uniform(splits[10], (ROWS, TOP), jnp.float32) ** shard_levels(splits[10], (ROWS, TOP), ((0, 64),), -0.2, 0.2)), 0.1, 1.0)
    w_gate = centred(splits[11], (EXPERTS, D, FF), D ** -0.5, 0.078125, ((0, 8), (2, 16)))
    w_up = centred(splits[12], (EXPERTS, D, FF), D ** -0.5, 0.078125, ((0, 8), (2, 16)))
    w_down = centred(splits[13], (EXPERTS, FF, D), FF ** -0.5, 0.0625, ((0, 8), (1, 16)))
    return {"queries": queries, "new_keys": new_keys, "new_values": new_values, "fork_map": fork_map, "key_cache": key_cache, "value_cache": value_cache, "cache_lengths": cache_lengths, "residual": residual, "norm_gain": norm_gain, "expert_ids": expert_ids, "gate_weights": gate_weights, "w_gate": w_gate, "w_up": w_up, "w_down": w_down}


def reference(queries, new_keys, new_values, fork_map, key_cache, value_cache, cache_lengths, residual, norm_gain, expert_ids, gate_weights, w_gate, w_up, w_down):
    group = QH // KVH
    scale = HD ** (-0.5)
    highest = lax.Precision.HIGHEST
    positions = jnp.arange(CACHE, dtype=jnp.int32)

    def attend(inputs):
        query_row, new_key, new_value, prompt = inputs
        keys = key_cache[prompt].astype(jnp.float32).reshape(CACHE, KVH, HD)
        values = value_cache[prompt].astype(jnp.float32).reshape(CACHE, KVH, HD)
        query_heads = query_row.astype(jnp.float32).reshape(KVH, group, HD)
        scores = jnp.einsum('hgd,thd->hgt', query_heads, keys, precision=highest) * scale
        valid = positions < cache_lengths[prompt]
        masked = jnp.where(valid, scores, -1e+30)
        own_score = jnp.einsum('hgd,hd->hg', query_heads, new_key.astype(jnp.float32).reshape(KVH, HD), precision=highest) * scale
        top = jnp.maximum(lax.optimization_barrier(jnp.max(masked, axis=-1)), own_score)
        raw = jnp.where(valid, jnp.exp(masked - top[..., None]), 0.0)
        own_weight = jnp.exp(own_score - top)
        total = lax.optimization_barrier(jnp.sum(raw, axis=-1)) + own_weight
        rounded = raw.astype(jnp.bfloat16).astype(jnp.float32)
        mixed = jnp.einsum('hgt,thd->hgd', rounded, values, precision=highest)
        mixed = mixed + own_weight[..., None] * new_value.astype(jnp.float32).reshape(KVH, 1, HD)
        return (mixed / total[..., None]).reshape(QH * HD).astype(jnp.bfloat16)
    attended = lax.map(attend, (queries, new_keys, new_values, fork_map))
    hidden_state = residual.astype(jnp.float32) + attended.astype(jnp.float32)
    meansq = lax.optimization_barrier(jnp.mean(hidden_state * hidden_state, axis=-1, keepdims=True))
    normed = (hidden_state * lax.rsqrt(meansq + 1e-05) * norm_gain.astype(jnp.float32)).astype(jnp.bfloat16)
    blocks = ROWS // ROW_DEV
    chosen = expert_ids.reshape(blocks, ROW_DEV * TOP)
    onehot = (chosen[:, :, None] == jnp.arange(EXPERTS, dtype=jnp.int32)[None, None, :]).astype(jnp.int32)
    ranks = lax.optimization_barrier(jnp.sum((jnp.cumsum(onehot, axis=1) - 1) * onehot, axis=2))
    block_ids = jnp.broadcast_to(jnp.arange(blocks, dtype=jnp.int32)[:, None], chosen.shape)
    row_ids = jnp.repeat(jnp.arange(ROWS, dtype=jnp.int32), TOP).reshape(blocks, ROW_DEV * TOP)
    table = jnp.full((EXPERTS, blocks, CAP), ROWS, jnp.int32).at[chosen, block_ids, ranks].set(row_ids)
    padded = jnp.concatenate([normed, jnp.zeros((1, D), jnp.bfloat16)], axis=0)

    def expert_rows(expert):
        picked = padded[table[expert].reshape(-1)]
        gate_part = jnp.dot(picked, w_gate[expert], preferred_element_type=jnp.float32)
        up_part = jnp.dot(picked, w_up[expert], preferred_element_type=jnp.float32)
        inner = (jax.nn.silu(gate_part) * up_part).astype(jnp.bfloat16)
        return jnp.dot(inner, w_down[expert], preferred_element_type=jnp.float32).astype(jnp.bfloat16)
    outputs = lax.map(expert_rows, jnp.arange(EXPERTS, dtype=jnp.int32))
    slots = (block_ids * CAP + ranks).reshape(-1)
    fetched = outputs[chosen.reshape(-1), slots].astype(jnp.float32).reshape(ROWS, TOP, D)
    combined = hidden_state + lax.optimization_barrier(jnp.sum(gate_weights[:, :, None] * fetched, axis=1))
    return combined.astype(jnp.bfloat16)
```

```python
import functools

import jax
import jax.numpy as jnp
from jax import lax
from jax.experimental import pallas as pl
from jax.experimental.pallas import tpu as pltpu
from jax.sharding import PartitionSpec as P

HD = 128
TOP = 2
CAP = 8
MESH = pl.DeviceIdType.MESH
F32 = jnp.float32
BF16 = jnp.bfloat16
VMEM = pltpu.VMEM


def attention_kernel(
    lens_ref, q_ref, nk_ref, nv_ref, fork_ref, k_ref, v_ref, o_ref, *, rows, group, prompts
):
    scale = HD ** (-0.5)
    cache_len = k_ref.shape[1]
    q_parts = [q_ref[:, g * HD : (g + 1) * HD] for g in range(group)]
    q = jnp.concatenate(q_parts, axis=0)
    new_key = jnp.concatenate([nk_ref[...].astype(F32)] * group, axis=0)
    new_value = jnp.concatenate([nv_ref[...].astype(F32)] * group, axis=0)
    prompt = jnp.concatenate([fork_ref[...] % prompts] * group, axis=0)
    own = jnp.sum(q.astype(F32) * new_key, axis=1, keepdims=True) * scale
    place = lax.broadcasted_iota(jnp.int32, (rows * group, cache_len), 1)
    masked = []
    top = own
    for p in range(prompts):
        score = (
            lax.dot_general(
                q, k_ref[p], (((1,), (1,)), ((), ())), preferred_element_type=F32
            )
            * scale
        )
        limit = jnp.where(prompt == p, lens_ref[p], 0)
        score = jnp.where(place < limit, score, -1e30)
        masked.append((score, place < limit))
        top = jnp.maximum(top, jnp.max(score, axis=1, keepdims=True))
    own_weight = jnp.exp(own - top)
    total = own_weight
    mixed = own_weight * new_value
    for p in range(prompts):
        score, live = masked[p]
        raw = jnp.where(live, jnp.exp(score - top), 0.0)
        total = total + jnp.sum(raw, axis=1, keepdims=True)
        mixed = mixed + jnp.dot(raw.astype(BF16), v_ref[p], preferred_element_type=F32)
    out = (mixed / total).astype(BF16)
    for g in range(group):
        o_ref[:, g * HD : (g + 1) * HD] = out[g * rows : (g + 1) * rows]


def attention(queries, new_keys, new_values, fork_map, key_cache, value_cache, cache_lengths):
    rows, width = queries.shape
    prompts, cache_len, kv_width = key_cache.shape
    heads = kv_width // HD
    group = width // kv_width
    return pl.pallas_call(
        functools.partial(attention_kernel, rows=rows, group=group, prompts=prompts),
        grid_spec=pltpu.PrefetchScalarGridSpec(
            num_scalar_prefetch=1,
            grid=(heads,),
            in_specs=[
                pl.BlockSpec((rows, group * HD), lambda i, s: (0, i)),
                pl.BlockSpec((rows, HD), lambda i, s: (0, i)),
                pl.BlockSpec((rows, HD), lambda i, s: (0, i)),
                pl.BlockSpec((rows, 1), lambda i, s: (0, 0)),
                pl.BlockSpec((prompts, cache_len, HD), lambda i, s: (0, 0, i)),
                pl.BlockSpec((prompts, cache_len, HD), lambda i, s: (0, 0, i)),
            ],
            out_specs=pl.BlockSpec((rows, group * HD), lambda i, s: (0, i)),
        ),
        out_shape=jax.ShapeDtypeStruct((rows, width), BF16),
        compiler_params=pltpu.CompilerParams(vmem_limit_bytes=32 * 2**20),
    )(
        cache_lengths,
        queries,
        new_keys,
        new_values,
        fork_map.reshape(rows, 1),
        key_cache,
        value_cache,
    )


def landed(ref, sem):
    pltpu.make_async_copy(ref, ref, sem).wait()


class Copies:
    def __init__(self, send_sems, recv_sems):
        self.send_sems, self.recv_sems, self.used = send_sems, recv_sems, 0

    def take(self, count=1):
        first = self.used
        self.used += count
        return first

    def send(self, index, src, dst, device):
        copy = pltpu.make_async_remote_copy(
            src_ref=src,
            dst_ref=dst,
            send_sem=self.send_sems.at[index],
            recv_sem=self.recv_sems.at[index],
            device_id=device,
            device_id_type=MESH,
        )
        copy.start()
        return copy

    def arrived(self, index, ref):
        landed(ref, self.recv_sems.at[index])


SEMS = 80


def expert_kernel(
    att_ref,
    res_ref,
    gain_ref,
    ids_ref,
    gw_ref,
    wg_hbm,
    wu_hbm,
    wd_hbm,
    o_ref,
    wg,
    wu,
    wd,
    ssq,
    hid,
    first,
    xb,
    zb,
    yb,
    h,
    g,
    gate,
    up,
    inner,
    part,
    r1p,
    r1m,
    r2p,
    r2m,
    zr,
    zf,
    q,
    t1p,
    t1m,
    t2p,
    t2m,
    xs,
    xr,
    last,
    send_sems,
    recv_sems,
    load_sems,
):
    c = lax.axis_index("pool")
    grp = lax.axis_index("grp")
    shard = lax.axis_index("shard")
    x, zl = grp // 2, grp % 2
    y, zh = shard // 2, shard % 2
    z = zh * 2 + zl
    rows, width = o_ref.shape
    half = width // 2
    hidden = wg.shape[1]

    def device(px, py, pz, pc=c):
        return (pc, px * 2 + pz % 2, py * 2 + pz // 2)

    def shift(a, d):
        return (a + d + 4) % 4

    other = device(x, y, z, 1 - c)
    y_up, y_down = device(x, shift(y, 1), z), device(x, shift(y, -1), z)
    x_to = [device(shift(x, d), y, z) for d in (1, 2, 3)]
    z_out = [shift(z, d) for d in (1, -1, 2)]
    z_in = [shift(z, d) for d in (-1, 1, 2)]
    z_to = [device(x, y, t) for t in z_out]
    y_of = [y, shift(y, -1), shift(y, 1), shift(y, 2)]
    mine = pl.ds(pl.multiple_of(c * half, half), half)
    theirs = pl.ds(pl.multiple_of((1 - c) * half, half), half)
    mine_hidden = pl.ds(pl.multiple_of(c * hidden, hidden), hidden)

    loads = [
        pltpu.make_async_copy(wg_hbm, wg, load_sems.at[0]),
        pltpu.make_async_copy(wu_hbm, wu, load_sems.at[1]),
        pltpu.make_async_copy(wd_hbm.at[:, mine], wd.at[mine_hidden], load_sems.at[2]),
    ]
    for load in loads:
        load.start()

    barrier = pltpu.get_barrier_semaphore()
    partners = [other, y_up, y_down] + x_to + z_to
    for partner in partners:
        pl.semaphore_signal(barrier, inc=1, device_id=partner, device_id_type=MESH)
    pl.semaphore_wait(barrier, len(partners))

    copies = Copies(send_sems, recv_sems)
    sent = []

    hidden_state = res_ref[:, mine].astype(F32) + att_ref[...].astype(F32)
    hid[...] = hidden_state
    square = jnp.sum(hidden_state * hidden_state, axis=1, keepdims=True)
    ssq[0] = jnp.broadcast_to(square, (rows, HD))
    s_ssq = copies.take()
    sent.append(copies.send(s_ssq, ssq.at[0], ssq.at[1], other))

    slots = xb.shape[0] * rows
    slot = lax.broadcasted_iota(jnp.int32, (rows, slots), 1)
    ids = ids_ref[...]
    pick_a = (ids[:, 0:1] == slot // CAP).astype(F32)
    pick_b = (ids[:, 1:2] == slot // CAP).astype(F32)
    before = (
        lax.broadcasted_iota(jnp.int32, (rows, rows), 1)
        < lax.broadcasted_iota(jnp.int32, (rows, rows), 0)
    ).astype(F32)
    rank = jnp.dot(before, pick_a + pick_b, preferred_element_type=F32)
    here = (rank == (slot % CAP).astype(F32)).astype(F32)
    placing = ((pick_a + pick_b) * here).astype(BF16)
    weighting = (pick_a * gw_ref[:, 0:1] + pick_b * gw_ref[:, 1:2]) * here

    copies.arrived(s_ssq, ssq.at[1])
    meansq = (ssq[0][:, 0:1] + ssq[1][:, 0:1]) / width
    normed = (hidden_state * lax.rsqrt(meansq + 1e-05) * gain_ref[:, mine].astype(F32)).astype(BF16)
    outgoing = lax.dot_general(
        placing, normed, (((0,), (0,)), ((), ())), preferred_element_type=F32
    )
    outgoing = outgoing.astype(BF16)
    for i in range(4):
        first[i] = outgoing[i * rows : (i + 1) * rows]

    s_x = copies.take(3)
    for i, d in enumerate((1, 2, 3)):
        sent.append(copies.send(s_x + i, first.at[shift(x, d)], xb.at[x], x_to[i]))
    xb[x] = first[x]
    s_wd = copies.take()
    sent.append(copies.send(s_wd, wd_hbm.at[:, theirs], wd.at[mine_hidden], other))
    for i, d in enumerate((1, 2, 3)):
        copies.arrived(s_x + i, xb.at[shift(x, -d)])

    def split_pairs(src, dst):
        for part_z in range(2):
            for pair in range(2):
                a = src[2 * pair].astype(F32)[part_z * CAP : (part_z + 1) * CAP]
                b = src[2 * pair + 1].astype(F32)[part_z * CAP : (part_z + 1) * CAP]
                dst[part_z, pair * 16 : (pair + 1) * 16] = jnp.concatenate([a, b], axis=0).astype(
                    BF16
                )

    def join_pairs(src, dst):
        for pair in range(2):
            a = src[0, pair * 16 : (pair + 1) * 16].astype(F32)
            b = src[1, pair * 16 : (pair + 1) * 16].astype(F32)
            dst[2 * pair] = jnp.concatenate([a[:CAP], b[:CAP]], axis=0).astype(BF16)
            dst[2 * pair + 1] = jnp.concatenate([a[CAP:], b[CAP:]], axis=0).astype(BF16)

    split_pairs(xb, zb)

    s_rows = copies.take(4)
    s_inner = copies.take(4)
    s_back = copies.take(3)
    s_last = copies.take()

    tile = 256

    def dots(rows_ref, k, weight_rows, add):
        block = y_of[k]

        @pl.loop(0, hidden // tile)
        def _(n):
            columns = pl.ds(pl.multiple_of(n * tile, tile), tile)
            data = rows_ref[block].reshape(-1, half)
            for weight, total in ((wg, gate), (wu, up)):
                value = jnp.dot(data, weight[weight_rows, columns], preferred_element_type=F32)
                if add:
                    value = value + total[k, :, columns]
                total[k, :, columns] = value

    def share_rows(k):
        return copies.send(s_rows + k, h.at[y_of[k]], g.at[y_of[k]], other)

    def own_half(k):
        dots(h, k, mine, False)

    def other_half(k):
        copies.arrived(s_rows + k, g.at[y_of[k]])
        dots(g, k, theirs, True)
        value = gate[k]
        inner[k, c] = (value / (1.0 + jnp.exp(-value)) * up[k]).astype(BF16)
        return copies.send(s_inner + k, inner.at[k, c], inner.at[k, c], other)

    def project(k):
        copies.arrived(s_inner + k, inner.at[k, 1 - c])
        block = y_of[k]

        @pl.loop(0, half // tile)
        def _(n):
            columns = pl.ds(pl.multiple_of(n * tile, tile), tile)
            value = jnp.dot(inner[k, 0], wd[0:hidden, columns], preferred_element_type=F32)
            value += jnp.dot(
                inner[k, 1], wd[hidden : 2 * hidden, columns], preferred_element_type=F32
            )
            part[block, :, :, columns] = value.astype(BF16).reshape(4, 32, tile)

    def load_wait():
        for load in loads[:2]:
            load.wait()

    def total_of(*refs):
        value = refs[0].astype(F32)
        for ref in refs[1:]:
            value = value + ref.astype(F32)
        return value.astype(BF16)

    def core_zero():
        own = []
        s_z = copies.take(3)
        for k in range(3):
            own.append(copies.send(s_z + k, zb.at[z_out[k] % 2], h.at[y, z], z_to[k]))
        h[y, z] = zb[z % 2]
        order = [z] + z_in
        s_up, s_down = copies.take(4), copies.take(4)
        for j in range(4):
            if j > 0:
                copies.arrived(s_z + j - 1, h.at[y, order[j]])
            block = h.at[y, order[j]]
            own.append(copies.send(s_up + j, block, block, y_up))
            own.append(copies.send(s_down + j, block, block, y_down))
        own.append(share_rows(0))
        s_up2, s_down2 = copies.take(4), copies.take(4)
        for j in range(4):
            copies.arrived(s_up + j, h.at[y_of[1], order[j]])
            block = h.at[y_of[1], order[j], 0:16]
            own.append(copies.send(s_up2 + j, block, block, y_up))
            copies.arrived(s_down + j, h.at[y_of[2], order[j]])
            block = h.at[y_of[2], order[j], 16:32]
            own.append(copies.send(s_down2 + j, block, block, y_down))
            if j == 0:
                load_wait()
                own_half(0)
            if j == 1:
                own.append(other_half(0))
        own.append(share_rows(1))
        own.append(share_rows(2))
        own_half(1)
        own_half(2)
        own.append(other_half(1))
        own.append(other_half(2))
        for j in range(4):
            copies.arrived(s_up2 + j, h.at[y_of[3], order[j], 0:16])
            copies.arrived(s_down2 + j, h.at[y_of[3], order[j], 16:32])
        own.append(share_rows(3))
        own_half(3)
        own.append(other_half(3))

        loads[2].wait()
        copies.arrived(s_wd, wd.at[pl.ds(pl.multiple_of((1 - c) * hidden, hidden), hidden)])
        back = z_out + [z]
        project(3)
        s_up, s_down = copies.take(4), copies.take(4)
        for j in range(4):
            block = part.at[y_of[3], back[j]]
            own.append(copies.send(s_up + j, block.at[0:16], r1p.at[back[j]], y_up))
            own.append(copies.send(s_down + j, block.at[16:32], r1m.at[back[j]], y_down))
        project(2)
        project(1)
        s_up2, s_down2 = copies.take(4), copies.take(4)
        for j in range(4):
            at = back[j]
            copies.arrived(s_up + j, r1p.at[at])
            part[y_of[2], at, 0:16] = total_of(part[y_of[2], at, 0:16], r1p[at])
            own.append(copies.send(s_up2 + j, part.at[y_of[2], at], r2p.at[at], y_up))
            copies.arrived(s_down + j, r1m.at[at])
            part[y_of[1], at, 16:32] = total_of(part[y_of[1], at, 16:32], r1m[at])
            own.append(copies.send(s_down2 + j, part.at[y_of[1], at], r2m.at[at], y_down))
        project(0)
        s_z = copies.take(3)
        for j in range(4):
            at = back[j]
            copies.arrived(s_up2 + j, r2p.at[at])
            copies.arrived(s_down2 + j, r2m.at[at])
            part[y, at] = total_of(part[y, at], r2p[at], r2m[at])
            if j < 3:
                own.append(copies.send(s_z + j, part.at[y, at], zr.at[j], z_to[j]))
        for j in range(3):
            copies.arrived(s_z + j, zr.at[j])
        q[0, z % 2] = total_of(part[y, z], zr[2])
        q[0, 1 - z % 2] = total_of(zr[0], zr[1])
        for copy in own:
            copy.wait_send()

    def core_one():
        own = []
        s_up, s_down = copies.take(), copies.take()
        own.append(copies.send(s_up, zb, yb.at[y], y_up))
        own.append(copies.send(s_down, zb, yb.at[y], y_down))
        s_z = copies.take(12)

        def spread(k, block):
            for j in range(3):
                own.append(
                    copies.send(
                        s_z + 3 * k + j, block.at[z_out[j] % 2], h.at[y_of[k], z], z_to[j]
                    )
                )
            h[y_of[k], z] = block[z % 2]

        def gathered(k):
            for j in range(3):
                copies.arrived(s_z + 3 * k + j, h.at[y_of[k], z_in[j]])

        spread(0, zb)
        s_up2, s_down2 = copies.take(), copies.take()
        copies.arrived(s_up, yb.at[y_of[1]])
        block = yb.at[y_of[1], 0]
        own.append(copies.send(s_up2, block, block, y_up))
        spread(1, yb.at[y_of[1]])
        copies.arrived(s_down, yb.at[y_of[2]])
        block = yb.at[y_of[2], 1]
        own.append(copies.send(s_down2, block, block, y_down))
        spread(2, yb.at[y_of[2]])
        gathered(0)
        own.append(share_rows(0))
        load_wait()
        own_half(0)
        copies.arrived(s_up2, yb.at[y_of[3], 0])
        copies.arrived(s_down2, yb.at[y_of[3], 1])
        spread(3, yb.at[y_of[3]])
        own.append(other_half(0))
        for k in (1, 2, 3):
            gathered(k)
            own.append(share_rows(k))
            own_half(k)
            own.append(other_half(k))

        loads[2].wait()
        copies.arrived(s_wd, wd.at[pl.ds(pl.multiple_of((1 - c) * hidden, hidden), hidden)])
        s_zf = copies.take(12)
        order = (3, 2, 1, 0)
        for k in order:
            project(k)
            for j in range(3):
                own.append(
                    copies.send(s_zf + 3 * k + j, part.at[y_of[k], z_out[j]], zf.at[k, j], z_to[j])
                )
        s_up, s_down = copies.take(), copies.take()
        s_up2, s_down2 = copies.take(), copies.take()
        for k in order:
            for j in range(3):
                copies.arrived(s_zf + 3 * k + j, zf.at[k, j])
            q[k, z % 2] = total_of(part[y_of[k], z], zf[k, 2])
            q[k, 1 - z % 2] = total_of(zf[k, 0], zf[k, 1])
            if k == 3:
                own.append(copies.send(s_up, q.at[3, 0], t1p, y_up))
                own.append(copies.send(s_down, q.at[3, 1], t1m, y_down))
            elif k == 2:
                copies.arrived(s_up, t1p)
                q[2, 0] = total_of(q[2, 0], t1p[...])
                own.append(copies.send(s_up2, q.at[2], t2p, y_up))
            elif k == 1:
                copies.arrived(s_down, t1m)
                q[1, 1] = total_of(q[1, 1], t1m[...])
                own.append(copies.send(s_down2, q.at[1], t2m, y_down))
        copies.arrived(s_up2, t2p)
        copies.arrived(s_down2, t2m)
        q[0] = total_of(q[0], t2p[...], t2m[...])
        for copy in own:
            copy.wait_send()

    common = copies.used
    pl.when(c == 0)(core_zero)
    used_zero, copies.used = copies.used, common
    pl.when(c == 1)(core_one)
    assert max(used_zero, copies.used) <= SEMS

    join_pairs(q.at[0], xs)
    for i, d in enumerate((1, 2, 3)):
        sent.append(copies.send(s_back + i, xs.at[shift(x, d)], xr.at[x], x_to[i]))
    xr[x] = xs[x]
    for i, d in enumerate((1, 2, 3)):
        copies.arrived(s_back + i, xr.at[shift(x, -d)])
    data = xr[...].reshape(slots, half)
    coarse = weighting.astype(BF16)
    fine = (weighting - coarse.astype(F32)).astype(BF16)
    result = jnp.dot(coarse, data, preferred_element_type=F32)
    result += jnp.dot(fine, data, preferred_element_type=F32)
    last[0] = (hid[...] + result).astype(BF16)
    sent.append(copies.send(s_last, last.at[0], last.at[1], other))
    o_ref[:, mine] = last[0]
    copies.arrived(s_last, last.at[1])
    o_ref[:, theirs] = last[1]
    for copy in sent:
        copy.wait_send()


def on_device(
    queries,
    new_keys,
    new_values,
    fork_map,
    key_cache,
    value_cache,
    cache_lengths,
    residual,
    norm_gain,
    expert_ids,
    gate_weights,
    w_gate,
    w_up,
    w_down,
):
    attended = attention(
        queries, new_keys, new_values, fork_map, key_cache, value_cache, cache_lengths
    )
    rows, width = residual.shape
    half = width // 2
    hidden = w_gate.shape[2]
    vmem = pl.BlockSpec(memory_space=VMEM)
    hbm = pl.BlockSpec(memory_space=pl.ANY)
    return pl.pallas_call(
        expert_kernel,
        out_shape=jax.ShapeDtypeStruct((rows, width), BF16),
        in_specs=[vmem] * 5 + [hbm] * 3,
        out_specs=vmem,
        scratch_shapes=[
            VMEM((width, hidden), BF16),
            VMEM((width, hidden), BF16),
            VMEM((2 * hidden, half), BF16),
            VMEM((2, rows, HD), F32),
            VMEM((rows, half), F32),
            VMEM((4, 16, half), BF16),
            VMEM((4, 16, half), BF16),
            VMEM((2, 32, half), BF16),
            VMEM((4, 2, 32, half), BF16),
            VMEM((4, 4, 32, half), BF16),
            VMEM((4, 4, 32, half), BF16),
            VMEM((4, 128, hidden), F32),
            VMEM((4, 128, hidden), F32),
            VMEM((4, 2, 128, hidden), BF16),
            VMEM((4, 4, 32, half), BF16),
            VMEM((4, 16, half), BF16),
            VMEM((4, 16, half), BF16),
            VMEM((4, 32, half), BF16),
            VMEM((4, 32, half), BF16),
            VMEM((3, 32, half), BF16),
            VMEM((4, 3, 32, half), BF16),
            VMEM((4, 2, 32, half), BF16),
            VMEM((32, half), BF16),
            VMEM((32, half), BF16),
            VMEM((2, 32, half), BF16),
            VMEM((2, 32, half), BF16),
            VMEM((4, 16, half), BF16),
            VMEM((4, 16, half), BF16),
            VMEM((2, rows, half), BF16),
            pltpu.SemaphoreType.DMA((SEMS,)),
            pltpu.SemaphoreType.DMA((SEMS,)),
            pltpu.SemaphoreType.DMA((3,)),
        ],
        compiler_params=pltpu.CompilerParams(
            collective_id=0, has_side_effects=True, vmem_limit_bytes=60 * 2**20
        ),
    )(
        attended,
        residual,
        norm_gain.reshape(1, width),
        expert_ids,
        gate_weights,
        w_gate[0],
        w_up[0],
        w_down[0],
    )


def solution(mesh):
    in_specs = (
        P(("grp", "shard"), "pool"),
        P(("grp", "shard"), "pool"),
        P(("grp", "shard"), "pool"),
        P(("grp", "shard")),
        P(("grp", "shard"), None, "pool"),
        P(("grp", "shard"), None, "pool"),
        P(("grp", "shard")),
        P(("grp", "shard"), None),
        P(),
        P(("grp", "shard"), None),
        P(("grp", "shard"), None),
        P("grp", None, ("pool", "shard")),
        P("grp", None, ("pool", "shard")),
        P("grp", ("pool", "shard"), None),
    )
    out_specs = P(("grp", "shard"), None)
    return jax.shard_map(
        on_device, mesh=mesh, in_specs=in_specs, out_specs=out_specs, check_vma=False
    )
```

```python
import math

import jax
import jax.numpy as jnp
from jax import lax
from jax.experimental import pallas as pl
from jax.experimental.pallas import tpu as pltpu
from jax.sharding import PartitionSpec as P

HD = 128
CAP = 8
MESH = pl.DeviceIdType.MESH
F32 = jnp.float32
BF16 = jnp.bfloat16
VMEM = pltpu.VMEM


def landed(ref, sem):
    pltpu.make_async_copy(ref, ref, sem).wait()


class Copies:
    def __init__(self, send_sems, recv_sems):
        self.send_sems, self.recv_sems, self.used = send_sems, recv_sems, 0

    def take(self, count=1):
        first = self.used
        self.used += count
        return first

    def send(self, index, src, dst, device):
        copy = pltpu.make_async_remote_copy(
            src_ref=src,
            dst_ref=dst,
            send_sem=self.send_sems.at[index],
            recv_sem=self.recv_sems.at[index],
            device_id=device,
            device_id_type=MESH,
        )
        copy.start()
        return copy

    def arrived(self, index, ref):
        landed(ref, self.recv_sems.at[index])


SEMS = 80


def layer_kernel(
    lens_ref,
    fork_ref,
    gain_ref,
    ids_ref,
    gw_ref,
    q_hbm,
    nk_hbm,
    nv_hbm,
    k_hbm,
    v_hbm,
    res_hbm,
    wg_hbm,
    wu_hbm,
    wd_hbm,
    o_ref,
    q_in,
    nk_in,
    nv_in,
    k_in,
    v_in,
    res_in,
    wg,
    wu,
    wd,
    ssq,
    hid,
    first,
    xb,
    zb,
    yb,
    h,
    g,
    gate,
    up,
    inner,
    part,
    r1p,
    r1m,
    r2p,
    r2m,
    zr,
    zf,
    q,
    t1p,
    t1m,
    t2p,
    t2m,
    xs,
    xr,
    last,
    send_sems,
    recv_sems,
    load_sems,
):
    c = lax.axis_index("pool")
    grp = lax.axis_index("grp")
    shard = lax.axis_index("shard")
    x, zl = grp // 2, grp % 2
    y, zh = shard // 2, shard % 2
    z = zh * 2 + zl
    rows, width = o_ref.shape
    half = width // 2
    hidden = wg.shape[1]

    def device(px, py, pz, pc=c):
        return (pc, px * 2 + pz % 2, py * 2 + pz // 2)

    def shift(a, d):
        return (a + d + 4) % 4

    other = device(x, y, z, 1 - c)
    y_up, y_down = device(x, shift(y, 1), z), device(x, shift(y, -1), z)
    x_to = [device(shift(x, d), y, z) for d in (1, 2, 3)]
    z_out = [shift(z, d) for d in (1, -1, 2)]
    z_to = [device(x, y, t) for t in z_out]
    mine = pl.ds(pl.multiple_of(c * half, half), half)
    theirs = pl.ds(pl.multiple_of((1 - c) * half, half), half)
    mine_hidden = pl.ds(pl.multiple_of(c * hidden, hidden), hidden)

    def load(index, src, dst):
        copy = pltpu.make_async_copy(src, dst, load_sems.at[index])
        copy.start()
        return copy

    heads = k_in.shape[0]
    group = half // (heads * HD)
    query_loads = [load(0, q_hbm, q_in), load(1, nk_hbm, nk_in), load(2, nv_hbm, nv_in)]
    cache_loads = []
    for head in range(heads):
        columns = slice(head * HD, (head + 1) * HD)
        cache_loads.append(
            (
                load(3 + 2 * head, k_hbm.at[:, :, columns], k_in.at[head]),
                load(4 + 2 * head, v_hbm.at[:, :, columns], v_in.at[head]),
            )
        )
    res_load = load(3 + 2 * heads, res_hbm.at[:, mine], res_in)
    loads = [
        load(4 + 2 * heads, wg_hbm, wg),
        load(5 + 2 * heads, wu_hbm, wu),
        load(6 + 2 * heads, wd_hbm.at[:, mine], wd.at[mine_hidden]),
    ]

    barrier = pltpu.get_barrier_semaphore()
    partners = [other, y_up, y_down] + x_to + z_to
    for partner in partners:
        pl.semaphore_signal(barrier, inc=1, device_id=partner, device_id_type=MESH)

    prompts, cache_len = k_in.shape[1], k_in.shape[2]
    diagonal = lax.broadcasted_iota(jnp.int32, (rows, rows), 0) == lax.broadcasted_iota(
        jnp.int32, (rows, rows), 1
    )
    prompt = jnp.sum(jnp.where(diagonal, fork_ref[...] % prompts, 0), axis=1, keepdims=True)
    prompt = jnp.concatenate([prompt] * group, axis=0)
    place = lax.broadcasted_iota(jnp.int32, (rows * group, cache_len), 1)
    limits = [jnp.where(prompt == p, lens_ref[p], 0) for p in range(prompts)]
    power = HD ** (-0.5) * math.log2(math.e)
    for query_load in query_loads:
        query_load.wait()
    attended = []
    for head in range(heads):
        at = head * group * HD
        queries = jnp.concatenate(
            [q_in[:, at + i * HD : at + (i + 1) * HD] for i in range(group)], axis=0
        )
        new_key = nk_in[:, head * HD : (head + 1) * HD].astype(F32)
        new_value = nv_in[:, head * HD : (head + 1) * HD].astype(F32)
        own = queries.astype(F32) * jnp.concatenate([new_key] * group, axis=0)
        own = jnp.sum(own, axis=1, keepdims=True)
        top = own
        scores = []
        cache_loads[head][0].wait()
        for p in range(prompts):
            score = lax.dot_general(
                queries, k_in[head, p], (((1,), (1,)), ((), ())), preferred_element_type=F32
            )
            score = jnp.where(place < limits[p], score, -1e30)
            scores.append(score)
            top = jnp.maximum(top, jnp.max(score, axis=1, keepdims=True))
        own_weight = jnp.exp2((own - top) * power)
        total = own_weight
        mixed = own_weight * jnp.concatenate([new_value] * group, axis=0)
        cache_loads[head][1].wait()
        for p in range(prompts):
            raw = jnp.exp2((scores[p] - top) * power)
            total = total + jnp.sum(raw, axis=1, keepdims=True)
            mixed = mixed + jnp.dot(
                raw.astype(BF16), v_in[head, p], preferred_element_type=F32
            )
        out = (mixed / total).astype(BF16).astype(F32)
        attended += [out[i * rows : (i + 1) * rows] for i in range(group)]
    attended = jnp.concatenate(attended, axis=1)

    slots = xb.shape[0] * rows
    slot = lax.broadcasted_iota(jnp.int32, (slots, rows), 0)
    pick_a = (ids_ref[0:1] == slot // CAP).astype(F32)
    pick_b = (ids_ref[1:2] == slot // CAP).astype(F32)
    before = (
        lax.broadcasted_iota(jnp.int32, (rows, rows), 0)
        < lax.broadcasted_iota(jnp.int32, (rows, rows), 1)
    ).astype(F32)
    rank = jnp.dot(pick_a + pick_b, before, preferred_element_type=F32)
    here = (rank == (slot % CAP).astype(F32)).astype(F32)
    placing = ((pick_a + pick_b) * here).astype(BF16)
    weighting = (pick_a * gw_ref[0:1] + pick_b * gw_ref[1:2]) * here
    gain = gain_ref[...].astype(F32)
    gain_rows = half // HD
    gain = jnp.where(c == 0, gain[:gain_rows], gain[gain_rows:])

    pl.semaphore_wait(barrier, len(partners))

    copies = Copies(send_sems, recv_sems)
    sent = []

    res_load.wait()
    hidden_state = res_in[...].astype(F32) + attended
    hid[...] = hidden_state
    square = jnp.sum(hidden_state * hidden_state, axis=1, keepdims=True)
    ssq[0] = jnp.broadcast_to(square, (rows, HD))
    s_ssq = copies.take()
    sent.append(copies.send(s_ssq, ssq.at[0], ssq.at[1], other))

    copies.arrived(s_ssq, ssq.at[1])
    meansq = (ssq[0][:, 0:1] + ssq[1][:, 0:1]) / width
    normed = hidden_state * lax.rsqrt(meansq + 1e-05)
    normed = jnp.concatenate(
        [normed[:, i * HD : (i + 1) * HD] * gain[i : i + 1] for i in range(gain_rows)], axis=1
    ).astype(BF16)
    outgoing = jnp.dot(placing, normed, preferred_element_type=F32)
    outgoing = outgoing.astype(BF16)
    for i in range(4):
        first[i] = outgoing[i * rows : (i + 1) * rows]

    s_x = copies.take(3)
    for i, d in enumerate((1, 2, 3)):
        sent.append(copies.send(s_x + i, first.at[shift(x, d)], xb.at[x], x_to[i]))
    xb[x] = first[x]
    def split_pairs(src, dst):
        for part_z in range(2):
            for pair in range(2):
                a = src[2 * pair].astype(F32)[part_z * CAP : (part_z + 1) * CAP]
                b = src[2 * pair + 1].astype(F32)[part_z * CAP : (part_z + 1) * CAP]
                dst[part_z, pair * 16 : (pair + 1) * 16] = jnp.concatenate([a, b], axis=0).astype(
                    BF16
                )

    def join_pairs(src, dst):
        for pair in range(2):
            a = src[0, pair * 16 : (pair + 1) * 16].astype(F32)
            b = src[1, pair * 16 : (pair + 1) * 16].astype(F32)
            dst[2 * pair] = jnp.concatenate([a[:CAP], b[:CAP]], axis=0).astype(BF16)
            dst[2 * pair + 1] = jnp.concatenate([a[CAP:], b[CAP:]], axis=0).astype(BF16)

    s_rows = copies.take(4)
    s_inner = copies.take(4)
    s_back = copies.take(3)
    s_last = copies.take()

    def dots(rows_ref, k, count, weight_rows, add):
        data = rows_ref[k : k + count].reshape(count * 128, half)
        for weight, total in ((wg, gate), (wu, up)):

            @pl.loop(0, hidden // 256)
            def _(n):
                columns = pl.ds(pl.multiple_of(n * 256, 256), 256)
                value = jnp.dot(data, weight[weight_rows, columns], preferred_element_type=F32)
                at = slice(k * 128, (k + count) * 128)
                if add:
                    value = value + total[at, columns]
                total[at, columns] = value

    def share_rows(k):
        return copies.send(s_rows + k, h.at[k], g.at[k], other)

    def own_half(k, count=1):
        dots(h, k, count, mine, False)

    def other_half(k, count=1):
        for i in range(k, k + count):
            copies.arrived(s_rows + i, g.at[i])
        dots(g, k, count, theirs, True)
        at = slice(k * 128, (k + count) * 128)
        value = gate[at]
        inner[c, at] = (value / (1.0 + jnp.exp(-value)) * up[at]).astype(BF16)
        block = inner.at[c, at]
        return copies.send(s_inner + k, block, block, other)

    def project(k, count=1):
        at = slice(k * 128, (k + count) * 128)
        copies.arrived(s_inner + k, inner.at[1 - c, at])

        @pl.loop(0, half // 1024)
        def _(n):
            columns = pl.ds(pl.multiple_of(n * 1024, 1024), 1024)
            value = jnp.dot(inner[0, at], wd[0:hidden, columns], preferred_element_type=F32)
            value += jnp.dot(
                inner[1, at], wd[hidden : 2 * hidden, columns], preferred_element_type=F32
            )
            part[k : k + count, :, :, columns] = value.astype(BF16).reshape(count, 4, 32, 1024)

    wd_pieces = 4
    s_wd = copies.take(wd_pieces)
    piece = hidden // wd_pieces

    def share_wd(i):
        rows_here = pl.ds(pl.multiple_of(c * hidden + i * piece, piece), piece)
        src = wd_hbm.at[i * piece : (i + 1) * piece, theirs]
        return copies.send(s_wd + i, src, wd.at[rows_here], other)

    def wd_wait():
        loads[2].wait()
        for i in range(wd_pieces):
            at = pl.multiple_of((1 - c) * hidden + i * piece, piece)
            copies.arrived(s_wd + i, wd.at[pl.ds(at, piece)])

    sent.append(share_wd(0))
    for i, d in enumerate((1, 2, 3)):
        copies.arrived(s_x + i, xb.at[shift(x, -d)])
    split_pairs(xb, zb)

    def load_wait():
        for load in loads[:2]:
            load.wait()

    def total_of(*refs):
        value = refs[0].astype(F32)
        for ref in refs[1:]:
            value = value + ref.astype(F32)
        return value.astype(BF16)

    def core_zero():
        own = []
        s_z = copies.take(3)
        for k in range(3):
            own.append(copies.send(s_z + k, zb.at[z_out[k] % 2], h.at[0, k + 1], z_to[k]))
        h[0, 0] = zb[z % 2]
        s_up, s_down = copies.take(4), copies.take(4)
        for j in range(4):
            if j > 0:
                copies.arrived(s_z + j - 1, h.at[0, j])
            own.append(copies.send(s_up + j, h.at[0, j], h.at[1, j], y_up))
            own.append(copies.send(s_down + j, h.at[0, j], h.at[2, j], y_down))
        own.append(share_rows(0))
        own.append(share_wd(1))
        s_up2, s_down2 = copies.take(4), copies.take(4)
        for j in range(4):
            copies.arrived(s_up + j, h.at[1, j])
            own.append(copies.send(s_up2 + j, h.at[1, j, 0:16], h.at[3, j, 0:16], y_up))
            copies.arrived(s_down + j, h.at[2, j])
            own.append(copies.send(s_down2 + j, h.at[2, j, 16:32], h.at[3, j, 16:32], y_down))
            if j == 0:
                load_wait()
                own_half(0)
            if j == 1:
                own.append(other_half(0))
                own.append(share_wd(2))
        own.append(share_rows(1))
        own.append(share_rows(2))
        own.append(share_wd(3))
        own_half(1, 2)
        own.append(other_half(1, 2))
        for j in range(4):
            copies.arrived(s_up2 + j, h.at[3, j, 0:16])
            copies.arrived(s_down2 + j, h.at[3, j, 16:32])
        own.append(share_rows(3))
        own_half(3)
        own.append(other_half(3))

        wd_wait()
        project(3)
        s_up, s_down = copies.take(4), copies.take(4)
        back = (2, 1, 3, 0)
        for j, at in enumerate(back):
            own.append(copies.send(s_up + j, part.at[3, at, 0:16], r1p.at[at], y_up))
            own.append(copies.send(s_down + j, part.at[3, at, 16:32], r1m.at[at], y_down))
        project(1, 2)
        s_up2, s_down2 = copies.take(4), copies.take(4)
        for j, at in enumerate(back):
            copies.arrived(s_up + j, r1p.at[at])
            part[2, at, 0:16] = total_of(part[2, at, 0:16], r1p[at])
            own.append(copies.send(s_up2 + j, part.at[2, at], r2p.at[at], y_up))
            copies.arrived(s_down + j, r1m.at[at])
            part[1, at, 16:32] = total_of(part[1, at, 16:32], r1m[at])
            own.append(copies.send(s_down2 + j, part.at[1, at], r2m.at[at], y_down))
        project(0)
        s_z = copies.take(3)
        for j, at in enumerate(back):
            copies.arrived(s_up2 + j, r2p.at[at])
            copies.arrived(s_down2 + j, r2m.at[at])
            part[0, at] = total_of(part[0, at], r2p[at], r2m[at])
            if j < 3:
                own.append(copies.send(s_z + j, part.at[0, at], zr.at[j], z_to[j]))
        for j in range(3):
            copies.arrived(s_z + j, zr.at[j])
        q[0, z % 2] = total_of(part[0, 0], zr[2])
        q[0, 1 - z % 2] = total_of(zr[0], zr[1])
        for copy in own:
            copy.wait_send()

    def core_one():
        own = []
        s_up, s_down = copies.take(), copies.take()
        own.append(copies.send(s_up, zb, yb.at[0], y_up))
        own.append(copies.send(s_down, zb, yb.at[1], y_down))
        s_z = copies.take(12)

        def spread(k, block):
            for j in range(3):
                own.append(
                    copies.send(
                        s_z + 3 * k + j, block.at[z_out[j] % 2], h.at[k, j + 1], z_to[j]
                    )
                )
            h[k, 0] = block[z % 2]

        def gathered(k):
            for j in range(3):
                copies.arrived(s_z + 3 * k + j, h.at[k, j + 1])

        spread(0, zb)
        s_up2, s_down2 = copies.take(), copies.take()
        copies.arrived(s_up, yb.at[0])
        own.append(copies.send(s_up2, yb.at[0, 0], yb.at[2, 0], y_up))
        spread(1, yb.at[0])
        copies.arrived(s_down, yb.at[1])
        own.append(copies.send(s_down2, yb.at[1, 1], yb.at[2, 1], y_down))
        spread(2, yb.at[1])
        gathered(0)
        own.append(share_rows(0))
        own.append(share_wd(1))
        load_wait()
        own_half(0)
        copies.arrived(s_up2, yb.at[2, 0])
        copies.arrived(s_down2, yb.at[2, 1])
        spread(3, yb.at[2])
        own.append(other_half(0))
        own.append(share_wd(2))
        gathered(1)
        own.append(share_rows(1))
        gathered(2)
        own.append(share_rows(2))
        own.append(share_wd(3))
        own_half(1, 2)
        own.append(other_half(1, 2))
        gathered(3)
        own.append(share_rows(3))
        own_half(3)
        own.append(other_half(3))

        wd_wait()
        s_zf = copies.take(12)
        order = (3, 2, 1, 0)

        def spread_back(k):
            for j, at in enumerate((2, 1, 3)):
                own.append(copies.send(s_zf + 3 * k + j, part.at[k, at], zf.at[k, j], z_to[j]))

        project(3)
        spread_back(3)
        project(1, 2)
        spread_back(2)
        spread_back(1)
        project(0)
        spread_back(0)
        s_up, s_down = copies.take(), copies.take()
        s_up2, s_down2 = copies.take(), copies.take()
        for k in order:
            for j in range(3):
                copies.arrived(s_zf + 3 * k + j, zf.at[k, j])
            q[k, z % 2] = total_of(part[k, 0], zf[k, 2])
            q[k, 1 - z % 2] = total_of(zf[k, 0], zf[k, 1])
            if k == 3:
                own.append(copies.send(s_up, q.at[3, 0], t1p, y_up))
                own.append(copies.send(s_down, q.at[3, 1], t1m, y_down))
            elif k == 2:
                copies.arrived(s_up, t1p)
                q[2, 0] = total_of(q[2, 0], t1p[...])
                own.append(copies.send(s_up2, q.at[2], t2p, y_up))
            elif k == 1:
                copies.arrived(s_down, t1m)
                q[1, 1] = total_of(q[1, 1], t1m[...])
                own.append(copies.send(s_down2, q.at[1], t2m, y_down))
        copies.arrived(s_up2, t2p)
        copies.arrived(s_down2, t2m)
        q[0] = total_of(q[0], t2p[...], t2m[...])
        for copy in own:
            copy.wait_send()

    common = copies.used
    pl.when(c == 0)(core_zero)
    used_zero, copies.used = copies.used, common
    pl.when(c == 1)(core_one)
    assert max(used_zero, copies.used) <= SEMS

    join_pairs(q.at[0], xs)
    for i, d in enumerate((1, 2, 3)):
        sent.append(copies.send(s_back + i, xs.at[shift(x, d)], xr.at[x], x_to[i]))
    xr[x] = xs[x]
    for i, d in enumerate((1, 2, 3)):
        copies.arrived(s_back + i, xr.at[shift(x, -d)])
    data = xr[...].reshape(slots, half)
    coarse = weighting.astype(BF16)
    fine = (weighting - coarse.astype(F32)).astype(BF16)
    over_slots = (((0,), (0,)), ((), ()))
    result = lax.dot_general(coarse, data, over_slots, preferred_element_type=F32)
    result += lax.dot_general(fine, data, over_slots, preferred_element_type=F32)
    last[0] = (hid[...] + result).astype(BF16)
    sent.append(copies.send(s_last, last.at[0], last.at[1], other))
    o_ref[:, mine] = last[0]
    copies.arrived(s_last, last.at[1])
    o_ref[:, theirs] = last[1]
    for copy in sent:
        copy.wait_send()


def on_device(
    queries,
    new_keys,
    new_values,
    fork_map,
    key_cache,
    value_cache,
    cache_lengths,
    residual,
    norm_gain,
    expert_ids,
    gate_weights,
    w_gate,
    w_up,
    w_down,
):
    rows, width = residual.shape
    half = width // 2
    hidden = w_gate.shape[2]
    prompts, cache_len, kv_width = key_cache.shape
    heads = kv_width // HD
    vmem = pl.BlockSpec(memory_space=VMEM)
    hbm = pl.BlockSpec(memory_space=pl.ANY)
    return pl.pallas_call(
        layer_kernel,
        out_shape=jax.ShapeDtypeStruct((rows, width), BF16),
        in_specs=[pl.BlockSpec(memory_space=pltpu.SMEM)] + [vmem] * 4 + [hbm] * 9,
        out_specs=vmem,
        scratch_shapes=[
            VMEM((rows, half), BF16),
            VMEM((rows, kv_width), BF16),
            VMEM((rows, kv_width), BF16),
            VMEM((heads, prompts, cache_len, HD), BF16),
            VMEM((heads, prompts, cache_len, HD), BF16),
            VMEM((rows, half), BF16),
            VMEM((width, hidden), BF16),
            VMEM((width, hidden), BF16),
            VMEM((2 * hidden, half), BF16),
            VMEM((2, rows, HD), F32),
            VMEM((rows, half), F32),
            VMEM((4, 16, half), BF16),
            VMEM((4, 16, half), BF16),
            VMEM((2, 32, half), BF16),
            VMEM((3, 2, 32, half), BF16),
            VMEM((4, 4, 32, half), BF16),
            VMEM((4, 4, 32, half), BF16),
            VMEM((512, hidden), F32),
            VMEM((512, hidden), F32),
            VMEM((2, 512, hidden), BF16),
            VMEM((4, 4, 32, half), BF16),
            VMEM((4, 16, half), BF16),
            VMEM((4, 16, half), BF16),
            VMEM((4, 32, half), BF16),
            VMEM((4, 32, half), BF16),
            VMEM((3, 32, half), BF16),
            VMEM((4, 3, 32, half), BF16),
            VMEM((4, 2, 32, half), BF16),
            VMEM((32, half), BF16),
            VMEM((32, half), BF16),
            VMEM((2, 32, half), BF16),
            VMEM((2, 32, half), BF16),
            VMEM((4, 16, half), BF16),
            VMEM((4, 16, half), BF16),
            VMEM((2, rows, half), BF16),
            pltpu.SemaphoreType.DMA((SEMS,)),
            pltpu.SemaphoreType.DMA((SEMS,)),
            pltpu.SemaphoreType.DMA((7 + 2 * heads,)),
        ],
        compiler_params=pltpu.CompilerParams(
            collective_id=0, has_side_effects=True, vmem_limit_bytes=60 * 2**20
        ),
    )(
        cache_lengths,
        fork_map.reshape(1, rows),
        norm_gain.reshape(width // HD, HD),
        expert_ids.T,
        gate_weights.T,
        queries,
        new_keys,
        new_values,
        key_cache,
        value_cache,
        residual,
        w_gate[0],
        w_up[0],
        w_down[0],
    )


def solution(mesh):
    in_specs = (
        P(("grp", "shard"), "pool"),
        P(("grp", "shard"), "pool"),
        P(("grp", "shard"), "pool"),
        P(("grp", "shard")),
        P(("grp", "shard"), None, "pool"),
        P(("grp", "shard"), None, "pool"),
        P(("grp", "shard")),
        P(("grp", "shard"), None),
        P(),
        P(("grp", "shard"), None),
        P(("grp", "shard"), None),
        P("grp", None, ("pool", "shard")),
        P("grp", None, ("pool", "shard")),
        P("grp", ("pool", "shard"), None),
    )
    out_specs = P(("grp", "shard"), None)
    return jax.shard_map(
        on_device, mesh=mesh, in_specs=in_specs, out_specs=out_specs, check_vma=False
    )
```

```python
import math

import jax
import jax.numpy as jnp
from jax import lax
from jax.experimental import pallas as pl
from jax.experimental.pallas import tpu as pltpu
from jax.sharding import PartitionSpec as P

HD = 128
CAP = 8
MESH = pl.DeviceIdType.MESH
F32 = jnp.float32
BF16 = jnp.bfloat16
VMEM = pltpu.VMEM


def landed(ref, sem):
    pltpu.make_async_copy(ref, ref, sem).wait()


class Copies:
    def __init__(self, send_sems, recv_sems):
        self.send_sems, self.recv_sems, self.used = send_sems, recv_sems, 0

    def take(self, count=1):
        first = self.used
        self.used += count
        return first

    def send(self, index, src, dst, device):
        copy = pltpu.make_async_remote_copy(
            src_ref=src,
            dst_ref=dst,
            send_sem=self.send_sems.at[index],
            recv_sem=self.recv_sems.at[index],
            device_id=device,
            device_id_type=MESH,
        )
        copy.start()
        return copy

    def arrived(self, index, ref):
        landed(ref, self.recv_sems.at[index])


SEMS = 112
WIDE = 2048


def layer_kernel(
    lens_ref,
    fork_ref,
    gain_ref,
    ids_ref,
    gw_ref,
    q_hbm,
    nk_hbm,
    nv_hbm,
    k_hbm,
    v_hbm,
    res_hbm,
    wg_hbm,
    wu_hbm,
    wd_hbm,
    o_ref,
    q_in,
    nk_in,
    nv_in,
    k_in,
    v_in,
    res_in,
    wg,
    wu,
    wd,
    ssq,
    hid,
    gate,
    up,
    inner,
    last,
    e_first,
    e_x,
    e_z,
    e_rows,
    e_part,
    e_up,
    e_down,
    e_up2,
    e_down2,
    e_zin,
    e_sum,
    e_back,
    e_end,
    f_first,
    f_x,
    f_z,
    f_y,
    f_rows,
    f_part,
    f_zin,
    f_sum,
    f_up,
    f_down,
    f_up2,
    f_down2,
    f_back,
    f_end,
    d_raw,
    d_weights,
    d_slots,
    d_rows,
    d_part,
    d_xin,
    d_group,
    d_zin,
    d_sum,
    d_yin,
    send_sems,
    recv_sems,
    load_sems,
    turn,
):
    c = lax.axis_index("pool")
    grp = lax.axis_index("grp")
    shard = lax.axis_index("shard")
    x, zl = grp // 2, grp % 2
    y, zh = shard // 2, shard % 2
    z = zh * 2 + zl
    rows, width = o_ref.shape
    half = width // 2
    hidden = wg.shape[1]

    def device(px, py, pz, pc=c):
        return (pc, px * 2 + pz % 2, py * 2 + pz // 2)

    def shift(a, d):
        return (a + d + 4) % 4

    other = device(x, y, z, 1 - c)
    x_out, y_out, z_out = ([shift(a, d) for d in (1, -1, 2)] for a in (x, y, z))
    x_to = [device(t, y, z) for t in x_out]
    y_to = [device(x, t, z) for t in y_out]
    z_to = [device(x, y, t) for t in z_out]
    y_up, y_down = y_to[:2]
    home = (1, 0, 2)
    mine = pl.ds(pl.multiple_of(c * half, half), half)
    theirs = pl.ds(pl.multiple_of((1 - c) * half, half), half)
    mine_hidden = pl.ds(pl.multiple_of(c * hidden, hidden), hidden)

    def load(index, src, dst):
        copy = pltpu.make_async_copy(src, dst, load_sems.at[index])
        copy.start()
        return copy

    heads = k_in.shape[0]
    group = half // (heads * HD)
    query_loads = [load(0, q_hbm, q_in), load(1, nk_hbm, nk_in), load(2, nv_hbm, nv_in)]
    cache_loads = []
    for head in range(heads):
        columns = slice(head * HD, (head + 1) * HD)
        cache_loads.append(
            (
                load(3 + 2 * head, k_hbm.at[:, :, columns], k_in.at[head]),
                load(4 + 2 * head, v_hbm.at[:, :, columns], v_in.at[head]),
            )
        )
    res_load = load(3 + 2 * heads, res_hbm.at[:, mine], res_in)
    loads = [
        load(4 + 2 * heads, wg_hbm, wg),
        load(5 + 2 * heads, wu_hbm, wu),
        load(6 + 2 * heads, wd_hbm.at[:, mine], wd.at[mine_hidden]),
    ]

    barrier = pltpu.get_barrier_semaphore()
    partners = [other] + x_to + y_to + z_to
    for partner in partners:
        pl.semaphore_signal(barrier, inc=1, device_id=partner, device_id_type=MESH)

    prompts, cache_len = k_in.shape[1], k_in.shape[2]
    diagonal = lax.broadcasted_iota(jnp.int32, (rows, rows), 0) == lax.broadcasted_iota(
        jnp.int32, (rows, rows), 1
    )
    prompt = jnp.sum(jnp.where(diagonal, fork_ref[...] % prompts, 0), axis=1, keepdims=True)
    prompt = jnp.concatenate([prompt] * group, axis=0)
    place = lax.broadcasted_iota(jnp.int32, (rows * group, cache_len), 1)
    limits = [jnp.where(prompt == p, lens_ref[p], 0) for p in range(prompts)]
    power = HD ** (-0.5) * math.log2(math.e)
    for query_load in query_loads:
        query_load.wait()
    attended = []
    for head in range(heads):
        at = head * group * HD
        queries = jnp.concatenate(
            [q_in[:, at + i * HD : at + (i + 1) * HD] for i in range(group)], axis=0
        )
        new_key = nk_in[:, head * HD : (head + 1) * HD].astype(F32)
        new_value = nv_in[:, head * HD : (head + 1) * HD].astype(F32)
        own = queries.astype(F32) * jnp.concatenate([new_key] * group, axis=0)
        own = jnp.sum(own, axis=1, keepdims=True)
        top = own
        scores = []
        cache_loads[head][0].wait()
        for p in range(prompts):
            score = lax.dot_general(
                queries, k_in[head, p], (((1,), (1,)), ((), ())), preferred_element_type=F32
            )
            score = jnp.where(place < limits[p], score, -1e30)
            scores.append(score)
            top = jnp.maximum(top, jnp.max(score, axis=1, keepdims=True))
        own_weight = jnp.exp2((own - top) * power)
        total = own_weight
        mixed = own_weight * jnp.concatenate([new_value] * group, axis=0)
        cache_loads[head][1].wait()
        for p in range(prompts):
            raw = jnp.exp2((scores[p] - top) * power)
            total = total + jnp.sum(raw, axis=1, keepdims=True)
            mixed = mixed + jnp.dot(
                raw.astype(BF16), v_in[head, p], preferred_element_type=F32
            )
        out = (mixed / total).astype(BF16).astype(F32)
        attended += [out[i * rows : (i + 1) * rows] for i in range(group)]
    attended = jnp.concatenate(attended, axis=1)

    slots = 4 * rows
    slot = lax.broadcasted_iota(jnp.int32, (slots, rows), 0)
    pick_a = (ids_ref[0:1] == slot // CAP).astype(F32)
    pick_b = (ids_ref[1:2] == slot // CAP).astype(F32)
    before = (
        lax.broadcasted_iota(jnp.int32, (rows, rows), 0)
        < lax.broadcasted_iota(jnp.int32, (rows, rows), 1)
    ).astype(F32)
    rank = jnp.dot(pick_a + pick_b, before, preferred_element_type=F32)
    here = (rank == (slot % CAP).astype(F32)).astype(F32)
    placing = ((pick_a + pick_b) * here).astype(BF16)
    weighting = (pick_a * gw_ref[0:1] + pick_b * gw_ref[1:2]) * here
    coarse = weighting.astype(BF16)
    fine = (weighting - coarse.astype(F32)).astype(BF16)
    gain = gain_ref[...].astype(F32)
    gain_rows = half // HD
    gain = jnp.where(c == 0, gain[:gain_rows], gain[gain_rows:])

    pl.semaphore_wait(barrier, len(partners))

    copies = Copies(send_sems, recv_sems)
    sent = []

    res_load.wait()
    hidden_state = res_in[...].astype(F32) + attended
    hid[...] = hidden_state
    square = jnp.sum(hidden_state * hidden_state, axis=1, keepdims=True)
    ssq[0] = jnp.broadcast_to(square, (rows, HD))
    s_ssq = copies.take()
    sent.append(copies.send(s_ssq, ssq.at[0], ssq.at[1], other))

    copies.arrived(s_ssq, ssq.at[1])
    meansq = (ssq[0][:, 0:1] + ssq[1][:, 0:1]) / width
    normed = hidden_state * lax.rsqrt(meansq + 1e-05)
    normed = jnp.concatenate(
        [normed[:, i * HD : (i + 1) * HD] * gain[i : i + 1] for i in range(gain_rows)], axis=1
    ).astype(BF16)
    over_rows = (((0,), (0,)), ((), ()))
    s_e, s_f, s_d = copies.take(4), copies.take(4), copies.take(4)
    s_inner = copies.take(4)
    s_last = copies.take()
    s_wd = copies.take()

    def split_pairs(src, dst):
        for part_z in range(2):
            for pair in range(2):
                a = src[2 * pair].astype(F32)[part_z * CAP : (part_z + 1) * CAP]
                b = src[2 * pair + 1].astype(F32)[part_z * CAP : (part_z + 1) * CAP]
                dst[part_z, pair * 16 : (pair + 1) * 16] = jnp.concatenate([a, b], axis=0).astype(
                    BF16
                )

    def join_pairs(src, dst):
        for pair in range(2):
            a = src[0, pair * 16 : (pair + 1) * 16].astype(F32)
            b = src[1, pair * 16 : (pair + 1) * 16].astype(F32)
            dst[2 * pair] = jnp.concatenate([a[:CAP], b[:CAP]], axis=0).astype(BF16)
            dst[2 * pair + 1] = jnp.concatenate([a[CAP:], b[CAP:]], axis=0).astype(BF16)

    def dots(data, weight_rows, put):
        for weight, total in ((wg, gate), (wu, up)):

            @pl.loop(0, hidden // 256)
            def _(n):
                columns = pl.ds(pl.multiple_of(n * 256, 256), 256)
                value = jnp.dot(data, weight[weight_rows, columns], preferred_element_type=F32)
                put(total, columns, value)

    def add_chunk(data, weight_rows, k, count):
        at = slice(k * 128, (k + count) * 128)

        def put(total, columns, value):
            total[at, columns] += value

        dots(data, weight_rows, put)

    def add_e(k, count=1):
        add_chunk(e_rows[k : k + count].reshape(count * 128, half), slice(0, half), k, count)

    def add_f(k, count=1):
        data = f_rows[k : k + count].reshape(count * 128, half - WIDE)
        add_chunk(data, slice(half + WIDE, width), k, count)

    def add_d(k, count=1):
        def put(total, columns, value):
            for i in range(count * 16):
                kz, kx, ky = k + i // 16, i // 4 % 4, i % 4
                at = kz * 128 + ky * 32 + kx * CAP
                total[at : at + CAP, columns] += value[i * CAP : (i + 1) * CAP]

        dots(d_rows[k : k + count].reshape(count * 128, WIDE), slice(half, half + WIDE), put)

    def share(first, ref, k):
        return copies.send(first + k, ref.at[k], ref.at[k], other)

    def shared(first, ref, k, count=1):
        for i in range(k, k + count):
            copies.arrived(first + i, ref.at[i])

    def share_wd():
        src = wd_hbm.at[:, theirs]
        return [copies.send(s_wd, src, wd.at[mine_hidden], other)]

    def wd_wait():
        loads[2].wait()
        at = pl.multiple_of((1 - c) * hidden, hidden)
        copies.arrived(s_wd, wd.at[pl.ds(at, hidden)])

    def load_wait():
        for load in loads[:2]:
            load.wait()

    def clear():
        gate[...] = jnp.zeros_like(gate)
        up[...] = jnp.zeros_like(up)

    def activate(k, count=1):
        at = slice(k * 128, (k + count) * 128)
        value = gate[at]
        inner[c, at] = (value / (1.0 + jnp.exp(-value)) * up[at]).astype(BF16)
        return copies.send(s_inner + k, inner.at[c, at], inner.at[c, at], other)

    def inner_wait(k, count=1):
        at = slice(k * 128, (k + count) * 128)
        copies.arrived(s_inner + k, inner.at[1 - c, at])

    def project(k, count, start, stop, put):
        at = slice(k * 128, (k + count) * 128)

        @pl.loop(0, (stop - start) // 1024)
        def _(n):
            columns = pl.ds(pl.multiple_of(start + n * 1024, 1024), 1024)
            value = jnp.dot(inner[0, at], wd[0:hidden, columns], preferred_element_type=F32)
            value += jnp.dot(
                inner[1, at], wd[hidden : 2 * hidden, columns], preferred_element_type=F32
            )
            put(n, value)

    def total_of(*refs):
        value = refs[0].astype(F32)
        for ref in refs[1:]:
            value = value + ref.astype(F32)
        return value.astype(BF16)

    def x_send(first, src, dst):
        done = []
        for i in range(3):
            done.append(copies.send(first + i, src.at[x_out[i]], dst.at[i + 1], x_to[i]))
        dst[0] = src[x]
        return done

    def x_return(first, src, dst):
        done = []
        for i in range(3):
            done.append(copies.send(first + i, src.at[i + 1], dst.at[x], x_to[home[i]]))
        dst[x] = src[0]
        return done

    def x_returned(first, dst):
        for i, d in enumerate((1, -1, 2)):
            copies.arrived(first + i, dst.at[shift(x, d)])

    def weighted(data):
        value = lax.dot_general(coarse, data, over_rows, preferred_element_type=F32)
        return value + lax.dot_general(fine, data, over_rows, preferred_element_type=F32)

    def place_slots(columns):
        return jnp.dot(placing, columns, preferred_element_type=F32).astype(BF16)

    def core_zero():
        own = []
        outgoing = place_slots(normed)
        for i in range(4):
            e_first[i] = outgoing[i * rows : (i + 1) * rows]
        s_x = copies.take(3)
        own += x_send(s_x, e_first, e_x)
        own += share_wd()
        clear()
        for i in range(3):
            copies.arrived(s_x + i, e_x.at[i + 1])
        split_pairs(e_x, e_z)
        s_z = copies.take(3)

        def to_z(k):
            return copies.send(s_z + k, e_z.at[z_out[k] % 2], e_rows.at[k + 1, 0], z_to[k])

        first_z = [to_z(0), to_z(1)]
        e_rows[0, 0] = e_z[z % 2]
        straight, straight_back = (0, 3), (3,)
        s_up, s_down, s_up2, s_down2 = (copies.take(4) for _ in range(4))

        def ring(j):
            if j > 0:
                copies.arrived(s_z + j - 1, e_rows.at[j, 0])
            own.append(copies.send(s_up + j, e_rows.at[j, 0], e_rows.at[j, 1], y_up))
            own.append(copies.send(s_down + j, e_rows.at[j, 0], e_rows.at[j, 2], y_down))
            if j in straight:
                own.append(copies.send(s_up2 + j, e_rows.at[j, 0], e_rows.at[j, 3], y_to[2]))

        def forward(j):
            if j in straight:
                return
            copies.arrived(s_up + j, e_rows.at[j, 1])
            own.append(
                copies.send(s_up2 + j, e_rows.at[j, 1, 0:16], e_rows.at[j, 3, 0:16], y_up)
            )
            copies.arrived(s_down + j, e_rows.at[j, 2])
            own.append(
                copies.send(s_down2 + j, e_rows.at[j, 2, 16:32], e_rows.at[j, 3, 16:32], y_down)
            )

        def ringed(j):
            if j in straight:
                copies.arrived(s_up + j, e_rows.at[j, 1])
                copies.arrived(s_down + j, e_rows.at[j, 2])
                copies.arrived(s_up2 + j, e_rows.at[j, 3])
            else:
                copies.arrived(s_up2 + j, e_rows.at[j, 3, 0:16])
                copies.arrived(s_down2 + j, e_rows.at[j, 3, 16:32])
            own.append(share(s_e, e_rows, j))

        s_bup, s_bdown, s_bup2, s_bdown2 = (copies.take(4) for _ in range(4))
        s_bz = copies.take(3)

        def project_e(k, count=1):
            inner_wait(k, count)

            def put(n, value):
                columns = pl.ds(pl.multiple_of(n * 1024, 1024), 1024)
                value = value.astype(BF16).reshape(count, 4, 32, 1024)
                e_part[k : k + count, :, :, columns] = value

            project(k, count, 0, half, put)
            for j in range(k, k + count):
                far_up, far_down = (y_to[2], y_to[2]) if j in straight_back else (y_up, y_down)
                own.append(copies.send(s_bup + j, e_part.at[j, 3, 0:16], e_up.at[j], far_up))
                own.append(
                    copies.send(s_bdown + j, e_part.at[j, 3, 16:32], e_down.at[j], far_down)
                )
                if j in straight_back:
                    own.append(copies.send(s_bup2 + j, e_part.at[j, 2], e_up2.at[j], y_up))
                    own.append(copies.send(s_bdown2 + j, e_part.at[j, 1], e_down2.at[j], y_down))

        def ring_back(j):
            if j in straight_back:
                return
            copies.arrived(s_bup + j, e_up.at[j])
            e_part[j, 2, 0:16] = total_of(e_part[j, 2, 0:16], e_up[j])
            own.append(copies.send(s_bup2 + j, e_part.at[j, 2], e_up2.at[j], y_up))
            copies.arrived(s_bdown + j, e_down.at[j])
            e_part[j, 1, 16:32] = total_of(e_part[j, 1, 16:32], e_down[j])
            own.append(copies.send(s_bdown2 + j, e_part.at[j, 1], e_down2.at[j], y_down))

        def ringed_back(j):
            copies.arrived(s_bup2 + j, e_up2.at[j])
            copies.arrived(s_bdown2 + j, e_down2.at[j])
            if j in straight_back:
                copies.arrived(s_bup + j, e_up.at[j])
                copies.arrived(s_bdown + j, e_down.at[j])
                e_part[j, 0, 0:16] = total_of(
                    e_part[j, 0, 0:16], e_up2[j, 0:16], e_down2[j, 0:16], e_up[j]
                )
                e_part[j, 0, 16:32] = total_of(
                    e_part[j, 0, 16:32], e_up2[j, 16:32], e_down2[j, 16:32], e_down[j]
                )
            else:
                e_part[j, 0] = total_of(e_part[j, 0], e_up2[j], e_down2[j])
            if j > 0:
                i = j - 1
                own.append(copies.send(s_bz + i, e_part.at[j, 0], e_zin.at[i], z_to[home[i]]))

        ring(0)
        for copy in first_z:
            copy.wait_send()
        last_z = to_z(2)
        forward(0)
        last_z.wait_send()
        pl.semaphore_signal(turn, inc=1, device_id=other, device_id_type=MESH)
        ring(1)
        ring(2)
        ringed(0)
        ring(3)
        load_wait()
        add_e(0)
        shared(s_d, d_rows, 0)
        add_d(0)
        shared(s_f, f_rows, 0)
        add_f(0)
        own.append(activate(0))
        forward(1)
        forward(2)
        wd_wait()
        project_e(0)
        forward(3)
        shared(s_d, d_rows, 1, 2)
        add_d(1, 2)
        shared(s_f, f_rows, 1, 2)
        add_f(1, 2)
        ringed(1)
        ringed(2)
        add_e(1, 2)
        own.append(activate(1, 2))
        ring_back(0)
        ringed(3)
        shared(s_d, d_rows, 3)
        add_d(3)
        shared(s_f, f_rows, 3)
        add_f(3)
        project_e(1, 2)
        add_e(3)
        own.append(activate(3))
        ring_back(1)
        ring_back(2)
        project_e(3)
        ringed_back(0)
        ringed_back(1)
        ringed_back(2)
        ring_back(3)
        ringed_back(3)
        for j in range(3):
            copies.arrived(s_bz + j, e_zin.at[j])
        e_sum[z % 2] = total_of(e_part[0, 0], e_zin[2])
        e_sum[1 - z % 2] = total_of(e_zin[0], e_zin[1])
        join_pairs(e_sum, e_back)
        s_x = copies.take(3)
        own += x_return(s_x, e_back, e_end)
        x_returned(s_x, e_end)
        last[...] = (hid[...] + weighted(e_end[...].reshape(slots, half))).astype(BF16)
        pltpu.make_async_copy(last, o_ref.at[:, mine], load_sems.at[0]).start()
        own.append(copies.send(s_last, last, o_ref.at[:, mine], other))
        for copy in own:
            copy.wait_send()

    def core_one():
        own = []
        eye = diagonal.astype(BF16)
        over_slots = (((1,), (1,)), ((), ()))
        for i, lanes in enumerate((coarse, fine)):
            lanes = lax.dot_general(eye, lanes, over_slots, preferred_element_type=F32)
            d_raw[0, 0, :, WIDE + i * slots : WIDE + (i + 1) * slots] = lanes.astype(BF16)
        d_raw[0, 0, :, 0:WIDE] = normed[:, 0:WIDE]
        s_dy, s_dz = copies.take(3), copies.take(12)
        for i in range(3):
            own.append(copies.send(s_dy + i, d_raw.at[0, 0], d_raw.at[0, i + 1], y_to[i]))

        def raw_to_z(ky, targets):
            for i in targets:
                own.append(
                    copies.send(
                        s_dz + 3 * ky + i, d_raw.at[0, ky], d_raw.at[i + 1, ky], z_to[i]
                    )
                )

        raw_to_z(0, (0, 1))
        outgoing = place_slots(normed[:, WIDE:])
        for i in range(4):
            f_first[i] = outgoing[i * rows : (i + 1) * rows]
        s_x = copies.take(3)
        own += x_send(s_x, f_first, f_x)
        own += share_wd()
        clear()
        for ky in (1, 2, 3):
            copies.arrived(s_dy + ky - 1, d_raw.at[0, ky])
            raw_to_z(ky, (0, 1))

        group_slots = 4 * 4 * CAP
        slot_in = lax.broadcasted_iota(jnp.int32, (slots, group_slots), 0)
        slot_at = lax.broadcasted_iota(jnp.int32, (slots, group_slots), 1)
        wanted = slot_at // (4 * CAP) * (2 * CAP) + zl * CAP + slot_at % CAP
        choose = (slot_in == wanted).astype(BF16)
        row_y = lax.broadcasted_iota(jnp.int32, (4 * rows, group_slots), 0) // rows
        slot_y = lax.broadcasted_iota(jnp.int32, (4 * rows, group_slots), 1) // CAP % 4
        same_y = row_y == slot_y
        s_dx = copies.take(12)

        def select(kz):
            if kz > 0:
                for ky in range(4):
                    copies.arrived(s_dz + 3 * ky + kz - 1, d_raw.at[kz, ky])
            for i in range(2):
                lanes = d_raw[kz, :, :, WIDE + i * slots : WIDE + (i + 1) * slots]
                lanes = jnp.dot(
                    lanes.reshape(4 * rows, slots), choose, preferred_element_type=F32
                )
                d_weights[kz, i] = jnp.where(same_y, lanes, 0.0).astype(BF16)
            chosen = (d_weights[kz, 0].astype(F32) > 0.0).astype(BF16)
            data = d_raw[kz, :, :, 0:WIDE].reshape(4 * rows, WIDE)
            value = lax.dot_general(chosen, data, over_rows, preferred_element_type=F32)
            d_slots[kz] = value.astype(BF16).reshape(4, 4 * CAP, WIDE)
            for i in range(3):
                own.append(
                    copies.send(
                        s_dx + 3 * kz + i, d_slots.at[kz, x_out[i]], d_rows.at[kz, i + 1], x_to[i]
                    )
                )
            d_rows[kz, 0] = d_slots[kz, x]

        def placed(kz):
            for i in range(3):
                copies.arrived(s_dx + 3 * kz + i, d_rows.at[kz, i + 1])
            own.append(share(s_d, d_rows, kz))

        select(0)
        for i in range(3):
            copies.arrived(s_x + i, f_x.at[i + 1])
        split_pairs(f_x, f_z)
        s_up, s_down = copies.take(), copies.take()
        own.append(copies.send(s_up, f_z, f_y.at[0], y_up))
        own.append(copies.send(s_down, f_z, f_y.at[1], y_down))
        s_z = copies.take(12)

        def spread(ky, block, targets):
            for j in targets:
                own.append(
                    copies.send(
                        s_z + 3 * ky + j, block.at[z_out[j] % 2], f_rows.at[j + 1, ky], z_to[j]
                    )
                )

        def gathered(kz):
            for ky in range(4):
                if kz > 0:
                    copies.arrived(s_z + 3 * ky + kz - 1, f_rows.at[kz, ky])
            own.append(share(s_f, f_rows, kz))

        s_bdx, s_bz, s_bdz = copies.take(12), copies.take(3), copies.take(3)

        def project_df(k, count=1):
            inner_wait(k, count)

            def put_d(n, value):
                columns = pl.ds(pl.multiple_of(n * 1024, 1024), 1024)
                for i in range(count):
                    for kx in range(4):
                        for ky in (0, 2):
                            at = i * 128 + ky * 32 + kx * CAP
                            pair = [value[at : at + CAP], value[at + 32 : at + 32 + CAP]]
                            d_part[k + i, kx, ky * CAP : (ky + 2) * CAP, columns] = (
                                jnp.concatenate(pair, axis=0).astype(BF16)
                            )

            def put_f(n, value):
                f_part[k : k + count] = value.astype(BF16).reshape(count, 4, 32, half - WIDE)

            project(k, count, 0, WIDE, put_d)
            for j in range(k, k + count):
                for i in range(3):
                    own.append(
                        copies.send(
                            s_bdx + 3 * j + i,
                            d_part.at[j, i + 1],
                            d_xin.at[j, x],
                            x_to[home[i]],
                        )
                    )
                d_xin[j, x] = d_part[j, 0]
            project(k, count, WIDE, half, put_f)
            for j in range(k, k + count):
                if j > 0:
                    i = j - 1
                    own.append(copies.send(s_bz + i, f_part.at[j], f_zin.at[i], z_to[home[i]]))

        def combine(kz):
            for i, d in enumerate((1, -1, 2)):
                copies.arrived(s_bdx + 3 * kz + i, d_xin.at[kz, shift(x, d)])
            data = d_xin[kz].reshape(group_slots, WIDE)
            value = jnp.dot(d_weights[kz, 0], data, preferred_element_type=F32)
            value += jnp.dot(d_weights[kz, 1], data, preferred_element_type=F32)
            d_group[kz] = value.astype(BF16)
            if kz > 0:
                i = kz - 1
                own.append(copies.send(s_bdz + i, d_group.at[kz], d_zin.at[i], z_to[home[i]]))

        select(1)
        select(2)
        s_up2, s_down2 = copies.take(), copies.take()
        copies.arrived(s_up, f_y.at[0])
        own.append(copies.send(s_up2, f_y.at[0, 0], f_y.at[2, 0], y_up))
        copies.arrived(s_down, f_y.at[1])
        own.append(copies.send(s_down2, f_y.at[1, 1], f_y.at[2, 1], y_down))
        pl.semaphore_wait(turn, 1)
        for ky in range(4):
            raw_to_z(ky, (2,))
        spread(0, f_z, (0, 1))
        spread(1, f_y.at[0], (0, 1))
        spread(2, f_y.at[1], (0, 1))
        f_rows[0, 0] = f_z[z % 2]
        f_rows[0, 1] = f_y[0, z % 2]
        f_rows[0, 2] = f_y[1, z % 2]
        placed(0)
        copies.arrived(s_up2, f_y.at[2, 0])
        copies.arrived(s_down2, f_y.at[2, 1])
        spread(3, f_y.at[2], (0, 1))
        f_rows[0, 3] = f_y[2, z % 2]
        gathered(0)
        for ky, block in enumerate((f_z, f_y.at[0], f_y.at[1], f_y.at[2])):
            spread(ky, block, (2,))
        load_wait()
        add_d(0)
        add_f(0)
        shared(s_e, e_rows, 0)
        add_e(0)
        own.append(activate(0))
        select(3)
        placed(1)
        placed(2)
        gathered(1)
        gathered(2)
        wd_wait()
        project_df(0)
        add_d(1, 2)
        add_f(1, 2)
        placed(3)
        gathered(3)
        shared(s_e, e_rows, 1, 2)
        add_e(1, 2)
        own.append(activate(1, 2))
        combine(0)
        add_d(3)
        project_df(1, 2)
        add_f(3)
        shared(s_e, e_rows, 3)
        add_e(3)
        own.append(activate(3))
        combine(1)
        combine(2)
        project_df(3)
        for i in range(3):
            copies.arrived(s_bz + i, f_zin.at[i])
        s_bup, s_bdown = copies.take(), copies.take()
        s_bup2, s_bdown2 = copies.take(), copies.take()
        for ky in (3, 2, 1, 0):
            f_sum[ky, z % 2] = total_of(f_part[0, ky], f_zin[2, ky])
            f_sum[ky, 1 - z % 2] = total_of(f_zin[0, ky], f_zin[1, ky])
            if ky == 3:
                own.append(copies.send(s_bup, f_sum.at[3, 0], f_up, y_up))
                own.append(copies.send(s_bdown, f_sum.at[3, 1], f_down, y_down))
        combine(3)
        copies.arrived(s_bup, f_up)
        f_sum[2, 0] = total_of(f_sum[2, 0], f_up[...])
        own.append(copies.send(s_bup2, f_sum.at[2], f_up2, y_up))
        copies.arrived(s_bdown, f_down)
        f_sum[1, 1] = total_of(f_sum[1, 1], f_down[...])
        own.append(copies.send(s_bdown2, f_sum.at[1], f_down2, y_down))
        for i in range(3):
            copies.arrived(s_bdz + i, d_zin.at[i])
        value = total_of(d_group[0], d_zin[0], d_zin[1], d_zin[2])
        d_sum[...] = value.reshape(4, rows, WIDE)
        s_dy = copies.take(3)
        for i in range(3):
            own.append(copies.send(s_dy + i, d_sum.at[i + 1], d_yin.at[i], y_to[home[i]]))
        copies.arrived(s_bup2, f_up2)
        copies.arrived(s_bdown2, f_down2)
        f_sum[0] = total_of(f_sum[0], f_up2[...], f_down2[...])
        join_pairs(f_sum.at[0], f_back)
        s_x = copies.take(3)
        own += x_return(s_x, f_back, f_end)
        x_returned(s_x, f_end)
        value = hid[:, WIDE:] + weighted(f_end[...].reshape(slots, half - WIDE))
        last[:, WIDE:] = value.astype(BF16)
        value = hid[:, 0:WIDE] + d_sum[0].astype(F32)
        for i in range(3):
            copies.arrived(s_dy + i, d_yin.at[i])
            value = value + d_yin[i].astype(F32)
        last[:, 0:WIDE] = value.astype(BF16)
        pltpu.make_async_copy(last, o_ref.at[:, mine], load_sems.at[0]).start()
        own.append(copies.send(s_last, last, o_ref.at[:, mine], other))
        for copy in own:
            copy.wait_send()

    common = copies.used
    pl.when(c == 0)(core_zero)
    used_zero, copies.used = copies.used, common
    pl.when(c == 1)(core_one)
    assert max(used_zero, copies.used) <= SEMS

    copies.arrived(s_last, o_ref.at[:, theirs])
    pltpu.make_async_copy(last, o_ref.at[:, mine], load_sems.at[0]).wait()
    for copy in sent:
        copy.wait_send()


def on_device(
    queries,
    new_keys,
    new_values,
    fork_map,
    key_cache,
    value_cache,
    cache_lengths,
    residual,
    norm_gain,
    expert_ids,
    gate_weights,
    w_gate,
    w_up,
    w_down,
):
    rows, width = residual.shape
    half = width // 2
    narrow = half - WIDE
    hidden = w_gate.shape[2]
    prompts, cache_len, kv_width = key_cache.shape
    heads = kv_width // HD
    vmem = pl.BlockSpec(memory_space=VMEM)
    hbm = pl.BlockSpec(memory_space=pl.ANY)
    return pl.pallas_call(
        layer_kernel,
        out_shape=jax.ShapeDtypeStruct((rows, width), BF16),
        in_specs=[pl.BlockSpec(memory_space=pltpu.SMEM)] + [vmem] * 4 + [hbm] * 9,
        out_specs=hbm,
        scratch_shapes=[
            VMEM((rows, half), BF16),
            VMEM((rows, kv_width), BF16),
            VMEM((rows, kv_width), BF16),
            VMEM((heads, prompts, cache_len, HD), BF16),
            VMEM((heads, prompts, cache_len, HD), BF16),
            VMEM((rows, half), BF16),
            VMEM((width, hidden), BF16),
            VMEM((width, hidden), BF16),
            VMEM((2 * hidden, half), BF16),
            VMEM((2, rows, HD), F32),
            VMEM((rows, half), F32),
            VMEM((512, hidden), F32),
            VMEM((512, hidden), F32),
            VMEM((2, 512, hidden), BF16),
            VMEM((rows, half), BF16),
            VMEM((4, 16, half), BF16),
            VMEM((4, 16, half), BF16),
            VMEM((2, 32, half), BF16),
            VMEM((4, 4, 32, half), BF16),
            VMEM((4, 4, 32, half), BF16),
            VMEM((4, 16, half), BF16),
            VMEM((4, 16, half), BF16),
            VMEM((4, 32, half), BF16),
            VMEM((4, 32, half), BF16),
            VMEM((3, 32, half), BF16),
            VMEM((2, 32, half), BF16),
            VMEM((4, 16, half), BF16),
            VMEM((4, 16, half), BF16),
            VMEM((4, 16, narrow), BF16),
            VMEM((4, 16, narrow), BF16),
            VMEM((2, 32, narrow), BF16),
            VMEM((3, 2, 32, narrow), BF16),
            VMEM((4, 4, 32, narrow), BF16),
            VMEM((4, 4, 32, narrow), BF16),
            VMEM((3, 4, 32, narrow), BF16),
            VMEM((4, 2, 32, narrow), BF16),
            VMEM((32, narrow), BF16),
            VMEM((32, narrow), BF16),
            VMEM((2, 32, narrow), BF16),
            VMEM((2, 32, narrow), BF16),
            VMEM((4, 16, narrow), BF16),
            VMEM((4, 16, narrow), BF16),
            VMEM((4, 4, rows, WIDE + HD), BF16),
            VMEM((4, 2, 4 * rows, HD), BF16),
            VMEM((4, 4, 32, WIDE), BF16),
            VMEM((4, 4, 32, WIDE), BF16),
            VMEM((4, 4, 32, WIDE), BF16),
            VMEM((4, 4, 32, WIDE), BF16),
            VMEM((4, 4 * rows, WIDE), BF16),
            VMEM((3, 4 * rows, WIDE), BF16),
            VMEM((4, rows, WIDE), BF16),
            VMEM((3, rows, WIDE), BF16),
            pltpu.SemaphoreType.DMA((SEMS,)),
            pltpu.SemaphoreType.DMA((SEMS,)),
            pltpu.SemaphoreType.DMA((7 + 2 * heads,)),
            pltpu.SemaphoreType.REGULAR,
        ],
        compiler_params=pltpu.CompilerParams(
            collective_id=0, has_side_effects=True, vmem_limit_bytes=60 * 2**20
        ),
    )(
        cache_lengths,
        fork_map.reshape(1, rows),
        norm_gain.reshape(width // HD, HD),
        expert_ids.T,
        gate_weights.T,
        queries,
        new_keys,
        new_values,
        key_cache,
        value_cache,
        residual,
        w_gate[0],
        w_up[0],
        w_down[0],
    )


def solution(mesh):
    in_specs = (
        P(("grp", "shard"), "pool"),
        P(("grp", "shard"), "pool"),
        P(("grp", "shard"), "pool"),
        P(("grp", "shard")),
        P(("grp", "shard"), None, "pool"),
        P(("grp", "shard"), None, "pool"),
        P(("grp", "shard")),
        P(("grp", "shard"), None),
        P(),
        P(("grp", "shard"), None),
        P(("grp", "shard"), None),
        P("grp", None, ("pool", "shard")),
        P("grp", None, ("pool", "shard")),
        P("grp", ("pool", "shard"), None),
    )
    out_specs = P(("grp", "shard"), None)
    return jax.shard_map(
        on_device, mesh=mesh, in_specs=in_specs, out_specs=out_specs, check_vma=False
    )
```

```python
import math

import jax
import jax.numpy as jnp
from jax import lax
from jax.experimental import pallas as pl
from jax.experimental.pallas import tpu as pltpu
from jax.sharding import PartitionSpec as P

HD = 128
CAP = 8
MESH = pl.DeviceIdType.MESH
F32 = jnp.float32
BF16 = jnp.bfloat16
VMEM = pltpu.VMEM


def landed(ref, sem):
    pltpu.make_async_copy(ref, ref, sem).wait()


class Copies:
    def __init__(self, send_sems, recv_sems):
        self.send_sems, self.recv_sems, self.used = send_sems, recv_sems, 0

    def take(self, count=1):
        first = self.used
        self.used += count
        return first

    def send(self, index, src, dst, device):
        copy = pltpu.make_async_remote_copy(
            src_ref=src,
            dst_ref=dst,
            send_sem=self.send_sems.at[index],
            recv_sem=self.recv_sems.at[index],
            device_id=device,
            device_id_type=MESH,
        )
        copy.start()
        return copy

    def arrived(self, index, ref):
        landed(ref, self.recv_sems.at[index])


SEMS = 112
WIDE = 2048


def layer_kernel(
    lens_ref,
    fork_ref,
    gain_ref,
    ids_ref,
    gw_ref,
    q_hbm,
    nk_hbm,
    nv_hbm,
    k_hbm,
    v_hbm,
    res_hbm,
    wg_hbm,
    wu_hbm,
    wd_hbm,
    o_ref,
    q_in,
    nk_in,
    nv_in,
    k_in,
    v_in,
    res_in,
    wg,
    wu,
    wd,
    ssq,
    hid,
    gate,
    up,
    inner,
    last,
    e_first,
    e_x,
    e_z,
    e_rows,
    e_part,
    e_up,
    e_down,
    e_up2,
    e_down2,
    e_zin,
    e_sum,
    e_back,
    e_end,
    f_first,
    f_x,
    f_z,
    f_y,
    f_rows,
    f_part,
    f_zin,
    f_sum,
    f_up,
    f_down,
    f_up2,
    f_down2,
    f_back,
    f_end,
    d_raw,
    d_weights,
    d_slots,
    d_rows,
    d_part,
    d_xin,
    d_group,
    d_zin,
    d_sum,
    d_yin,
    send_sems,
    recv_sems,
    load_sems,
    turn,
):
    c = lax.axis_index("pool")
    grp = lax.axis_index("grp")
    shard = lax.axis_index("shard")
    x, zl = grp // 2, grp % 2
    y, zh = shard // 2, shard % 2
    z = zh * 2 + zl
    rows, width = o_ref.shape
    half = width // 2
    hidden = wg.shape[1]

    def device(px, py, pz, pc=c):
        return (pc, px * 2 + pz % 2, py * 2 + pz // 2)

    def shift(a, d):
        return (a + d + 4) % 4

    other = device(x, y, z, 1 - c)
    x_out, y_out, z_out = ([shift(a, d) for d in (1, -1, 2)] for a in (x, y, z))
    x_to = [device(t, y, z) for t in x_out]
    y_to = [device(x, t, z) for t in y_out]
    z_to = [device(x, y, t) for t in z_out]
    y_up, y_down = y_to[:2]
    home = (1, 0, 2)
    mine = pl.ds(pl.multiple_of(c * half, half), half)
    theirs = pl.ds(pl.multiple_of((1 - c) * half, half), half)
    mine_hidden = pl.ds(pl.multiple_of(c * hidden, hidden), hidden)

    def load(index, src, dst):
        copy = pltpu.make_async_copy(src, dst, load_sems.at[index])
        copy.start()
        return copy

    heads = k_in.shape[0]
    group = half // (heads * HD)
    query_loads = [load(0, q_hbm, q_in), load(1, nk_hbm, nk_in), load(2, nv_hbm, nv_in)]
    cache_loads = []
    for head in range(heads):
        columns = slice(head * HD, (head + 1) * HD)
        cache_loads.append(
            (
                load(3 + 2 * head, k_hbm.at[:, :, columns], k_in.at[head]),
                load(4 + 2 * head, v_hbm.at[:, :, columns], v_in.at[head]),
            )
        )
    res_load = load(3 + 2 * heads, res_hbm.at[:, mine], res_in)
    barrier = pltpu.get_barrier_semaphore()
    partners = [other] + x_to + y_to + z_to
    for partner in partners:
        pl.semaphore_signal(barrier, inc=1, device_id=partner, device_id_type=MESH)

    prompts, cache_len = k_in.shape[1], k_in.shape[2]
    diagonal = lax.broadcasted_iota(jnp.int32, (rows, rows), 0) == lax.broadcasted_iota(
        jnp.int32, (rows, rows), 1
    )
    prompt = jnp.sum(jnp.where(diagonal, fork_ref[...] % prompts, 0), axis=1, keepdims=True)
    prompt = jnp.concatenate([prompt] * group, axis=0)
    place = lax.broadcasted_iota(jnp.int32, (rows * group, cache_len), 1)
    limits = [jnp.where(prompt == p, lens_ref[p], 0) for p in range(prompts)]
    power = HD ** (-0.5) * math.log2(math.e)
    for query_load in query_loads:
        query_load.wait()
    attended = []
    for head in range(heads):
        at = head * group * HD
        queries = jnp.concatenate(
            [q_in[:, at + i * HD : at + (i + 1) * HD] for i in range(group)], axis=0
        )
        new_key = nk_in[:, head * HD : (head + 1) * HD].astype(F32)
        new_value = nv_in[:, head * HD : (head + 1) * HD].astype(F32)
        own = queries.astype(F32) * jnp.concatenate([new_key] * group, axis=0)
        own = jnp.sum(own, axis=1, keepdims=True)
        top = own
        scores = []
        cache_loads[head][0].wait()
        for p in range(prompts):
            score = lax.dot_general(
                queries, k_in[head, p], (((1,), (1,)), ((), ())), preferred_element_type=F32
            )
            score = jnp.where(place < limits[p], score, -1e30)
            scores.append(score)
            top = jnp.maximum(top, jnp.max(score, axis=1, keepdims=True))
        own_weight = jnp.exp2((own - top) * power)
        total = own_weight
        mixed = own_weight * jnp.concatenate([new_value] * group, axis=0)
        cache_loads[head][1].wait()
        for p in range(prompts):
            raw = jnp.exp2((scores[p] - top) * power)
            total = total + jnp.sum(raw, axis=1, keepdims=True)
            mixed = mixed + jnp.dot(
                raw.astype(BF16), v_in[head, p], preferred_element_type=F32
            )
        out = (mixed / total).astype(BF16).astype(F32)
        attended += [out[i * rows : (i + 1) * rows] for i in range(group)]
    attended = jnp.concatenate(attended, axis=1)
    loads = [
        load(4 + 2 * heads, wg_hbm, wg),
        load(5 + 2 * heads, wu_hbm, wu),
        load(6 + 2 * heads, wd_hbm.at[:, mine], wd.at[mine_hidden]),
    ]

    slots = 4 * rows
    slot = lax.broadcasted_iota(jnp.int32, (slots, rows), 0)
    pick_a = (ids_ref[0:1] == slot // CAP).astype(F32)
    pick_b = (ids_ref[1:2] == slot // CAP).astype(F32)
    before = (
        lax.broadcasted_iota(jnp.int32, (rows, rows), 0)
        < lax.broadcasted_iota(jnp.int32, (rows, rows), 1)
    ).astype(F32)
    rank = jnp.dot(pick_a + pick_b, before, preferred_element_type=F32)
    here = (rank == (slot % CAP).astype(F32)).astype(F32)
    placing = ((pick_a + pick_b) * here).astype(BF16)
    weighting = (pick_a * gw_ref[0:1] + pick_b * gw_ref[1:2]) * here
    coarse = weighting.astype(BF16)
    fine = (weighting - coarse.astype(F32)).astype(BF16)
    gain = gain_ref[...].astype(F32)
    gain_rows = half // HD
    gain = jnp.where(c == 0, gain[:gain_rows], gain[gain_rows:])

    pl.semaphore_wait(barrier, len(partners))

    copies = Copies(send_sems, recv_sems)
    sent = []

    res_load.wait()
    hidden_state = res_in[...].astype(F32) + attended
    hid[...] = hidden_state
    square = jnp.sum(hidden_state * hidden_state, axis=1, keepdims=True)
    ssq[0] = jnp.broadcast_to(square, (rows, HD))
    s_ssq = copies.take()
    sent.append(copies.send(s_ssq, ssq.at[0], ssq.at[1], other))

    copies.arrived(s_ssq, ssq.at[1])
    meansq = (ssq[0][:, 0:1] + ssq[1][:, 0:1]) / width
    normed = hidden_state * lax.rsqrt(meansq + 1e-05)
    normed = jnp.concatenate(
        [normed[:, i * HD : (i + 1) * HD] * gain[i : i + 1] for i in range(gain_rows)], axis=1
    ).astype(BF16)
    over_rows = (((0,), (0,)), ((), ()))
    s_e, s_f, s_d = copies.take(4), copies.take(4), copies.take(4)
    s_inner = copies.take(4)
    s_last = copies.take()
    s_wd = copies.take()

    def split_pairs(src, dst):
        for part_z in range(2):
            for pair in range(2):
                a = src[2 * pair].astype(F32)[part_z * CAP : (part_z + 1) * CAP]
                b = src[2 * pair + 1].astype(F32)[part_z * CAP : (part_z + 1) * CAP]
                dst[part_z, pair * 16 : (pair + 1) * 16] = jnp.concatenate([a, b], axis=0).astype(
                    BF16
                )

    def join_pairs(src, dst):
        for pair in range(2):
            a = src[0, pair * 16 : (pair + 1) * 16].astype(F32)
            b = src[1, pair * 16 : (pair + 1) * 16].astype(F32)
            dst[2 * pair] = jnp.concatenate([a[:CAP], b[:CAP]], axis=0).astype(BF16)
            dst[2 * pair + 1] = jnp.concatenate([a[CAP:], b[CAP:]], axis=0).astype(BF16)

    def dots(parts, put, step):
        for weight, total in ((wg, gate), (wu, up)):

            @pl.loop(0, hidden // step)
            def _(n):
                columns = pl.ds(pl.multiple_of(n * step, step), step)
                value = None
                for data, weight_rows in parts:
                    term = jnp.dot(data, weight[weight_rows, columns], preferred_element_type=F32)
                    value = term if value is None else value + term
                put(total, columns, value)

    def e_of(k, count):
        return e_rows[k : k + count].reshape(count * 128, half), slice(0, half)

    def f_of(k, count):
        data = f_rows[k : k + count].reshape(count * 128, half - WIDE)
        return data, slice(half + WIDE, width)

    def add_ef(k, count, use_e, use_f, write):
        at = slice(k * 128, (k + count) * 128)
        parts = [e_of(k, count)] * use_e + [f_of(k, count)] * use_f

        def put(total, columns, value):
            if write:
                total[at, columns] = value
            else:
                total[at, columns] += value

        dots(parts, put, 256)

    def add_d(k, count, write):
        def put(total, columns, value):
            for i in range(count * 16):
                kz, kx, ky = k + i // 16, i // 4 % 4, i % 4
                at = kz * 128 + ky * 32 + kx * CAP
                rows_here = value[i * CAP : (i + 1) * CAP]
                if write:
                    total[at : at + CAP, columns] = rows_here
                else:
                    total[at : at + CAP, columns] += rows_here

        data = d_rows[k : k + count].reshape(count * 128, WIDE)
        dots([(data, slice(half, half + WIDE))], put, 256)

    def share(first, ref, k):
        return copies.send(first + k, ref.at[k], ref.at[k], other)

    def shared(first, ref, k, count=1):
        for i in range(k, k + count):
            copies.arrived(first + i, ref.at[i])

    def share_wd():
        src = wd_hbm.at[:, theirs]
        return [copies.send(s_wd, src, wd.at[mine_hidden], other)]

    def wd_wait():
        loads[2].wait()
        at = pl.multiple_of((1 - c) * hidden, hidden)
        copies.arrived(s_wd, wd.at[pl.ds(at, hidden)])

    def load_wait():
        for load in loads[:2]:
            load.wait()

    def activate(k, count=1):
        at = slice(k * 128, (k + count) * 128)
        value = gate[at]
        inner[c, at] = (value / (1.0 + jnp.exp(-value)) * up[at]).astype(BF16)
        return copies.send(s_inner + k, inner.at[c, at], inner.at[c, at], other)

    def inner_wait(k, count=1):
        at = slice(k * 128, (k + count) * 128)
        copies.arrived(s_inner + k, inner.at[1 - c, at])

    def project(k, count, start, stop, put):
        at = slice(k * 128, (k + count) * 128)

        @pl.loop(0, (stop - start) // 1024)
        def _(n):
            columns = pl.ds(pl.multiple_of(start + n * 1024, 1024), 1024)
            value = jnp.dot(inner[0, at], wd[0:hidden, columns], preferred_element_type=F32)
            value += jnp.dot(
                inner[1, at], wd[hidden : 2 * hidden, columns], preferred_element_type=F32
            )
            put(n, value)

    def total_of(*refs):
        value = refs[0].astype(F32)
        for ref in refs[1:]:
            value = value + ref.astype(F32)
        return value.astype(BF16)

    def x_send(first, src, dst):
        done = []
        for i in range(3):
            done.append(copies.send(first + i, src.at[x_out[i]], dst.at[i + 1], x_to[i]))
        dst[0] = src[x]
        return done

    def x_return(first, src, dst):
        done = []
        for i in range(3):
            done.append(copies.send(first + i, src.at[i + 1], dst.at[x], x_to[home[i]]))
        dst[x] = src[0]
        return done

    def x_returned(first, dst):
        for i, d in enumerate((1, -1, 2)):
            copies.arrived(first + i, dst.at[shift(x, d)])

    def weighted(data):
        value = lax.dot_general(coarse, data, over_rows, preferred_element_type=F32)
        return value + lax.dot_general(fine, data, over_rows, preferred_element_type=F32)

    def place_slots(columns):
        return jnp.dot(placing, columns, preferred_element_type=F32).astype(BF16)

    def core_zero():
        own = []
        outgoing = place_slots(normed)
        for i in range(4):
            e_first[i] = outgoing[i * rows : (i + 1) * rows]
        s_x = copies.take(3)
        own += x_send(s_x, e_first, e_x)
        own += share_wd()
        for i in range(3):
            copies.arrived(s_x + i, e_x.at[i + 1])
        split_pairs(e_x, e_z)
        s_z = copies.take(3)

        def to_z(k):
            return copies.send(s_z + k, e_z.at[z_out[k] % 2], e_rows.at[k + 1, 0], z_to[k])

        first_z = [to_z(0), to_z(1)]
        e_rows[0, 0] = e_z[z % 2]
        straight, straight_back = (0, 3), (0, 1, 2, 3)
        s_up, s_down, s_up2, s_down2 = (copies.take(4) for _ in range(4))

        def ring(j):
            if j > 0:
                copies.arrived(s_z + j - 1, e_rows.at[j, 0])
            own.append(copies.send(s_up + j, e_rows.at[j, 0], e_rows.at[j, 1], y_up))
            own.append(copies.send(s_down + j, e_rows.at[j, 0], e_rows.at[j, 2], y_down))
            if j in straight:
                own.append(copies.send(s_up2 + j, e_rows.at[j, 0], e_rows.at[j, 3], y_to[2]))

        def forward(j):
            if j in straight:
                return
            copies.arrived(s_up + j, e_rows.at[j, 1])
            own.append(
                copies.send(s_up2 + j, e_rows.at[j, 1, 0:16], e_rows.at[j, 3, 0:16], y_up)
            )
            copies.arrived(s_down + j, e_rows.at[j, 2])
            own.append(
                copies.send(s_down2 + j, e_rows.at[j, 2, 16:32], e_rows.at[j, 3, 16:32], y_down)
            )

        def ringed(j):
            if j in straight:
                copies.arrived(s_up + j, e_rows.at[j, 1])
                copies.arrived(s_down + j, e_rows.at[j, 2])
                copies.arrived(s_up2 + j, e_rows.at[j, 3])
            else:
                copies.arrived(s_up2 + j, e_rows.at[j, 3, 0:16])
                copies.arrived(s_down2 + j, e_rows.at[j, 3, 16:32])
            own.append(share(s_e, e_rows, j))

        s_bup, s_bdown, s_bup2, s_bdown2 = (copies.take(4) for _ in range(4))
        s_bz = copies.take(3)

        def project_e(k, count=1):
            inner_wait(k, count)

            def put(n, value):
                columns = pl.ds(pl.multiple_of(n * 1024, 1024), 1024)
                value = value.astype(BF16).reshape(count, 4, 32, 1024)
                e_part[k : k + count, :, :, columns] = value

            project(k, count, 0, half, put)
            for j in range(k, k + count):
                far_up, far_down = (y_to[2], y_to[2]) if j in straight_back else (y_up, y_down)
                own.append(copies.send(s_bup + j, e_part.at[j, 3, 0:16], e_up.at[j], far_up))
                own.append(
                    copies.send(s_bdown + j, e_part.at[j, 3, 16:32], e_down.at[j], far_down)
                )
                if j in straight_back:
                    own.append(copies.send(s_bup2 + j, e_part.at[j, 2], e_up2.at[j], y_up))
                    own.append(copies.send(s_bdown2 + j, e_part.at[j, 1], e_down2.at[j], y_down))

        def ring_back(j):
            if j in straight_back:
                return
            copies.arrived(s_bup + j, e_up.at[j])
            e_part[j, 2, 0:16] = total_of(e_part[j, 2, 0:16], e_up[j])
            own.append(copies.send(s_bup2 + j, e_part.at[j, 2], e_up2.at[j], y_up))
            copies.arrived(s_bdown + j, e_down.at[j])
            e_part[j, 1, 16:32] = total_of(e_part[j, 1, 16:32], e_down[j])
            own.append(copies.send(s_bdown2 + j, e_part.at[j, 1], e_down2.at[j], y_down))

        def ringed_back(j):
            copies.arrived(s_bup2 + j, e_up2.at[j])
            copies.arrived(s_bdown2 + j, e_down2.at[j])
            if j in straight_back:
                copies.arrived(s_bup + j, e_up.at[j])
                copies.arrived(s_bdown + j, e_down.at[j])
                e_part[j, 0, 0:16] = total_of(
                    e_part[j, 0, 0:16], e_up2[j, 0:16], e_down2[j, 0:16], e_up[j]
                )
                e_part[j, 0, 16:32] = total_of(
                    e_part[j, 0, 16:32], e_up2[j, 16:32], e_down2[j, 16:32], e_down[j]
                )
            else:
                e_part[j, 0] = total_of(e_part[j, 0], e_up2[j], e_down2[j])
            if j > 0:
                i = j - 1
                own.append(copies.send(s_bz + i, e_part.at[j, 0], e_zin.at[i], z_to[home[i]]))

        ring(0)
        for copy in first_z:
            copy.wait_send()
        last_z = to_z(2)
        forward(0)
        last_z.wait_send()
        pl.semaphore_signal(turn, inc=1, device_id=other, device_id_type=MESH)
        ring(1)
        ring(2)
        ringed(0)
        load_wait()
        add_ef(0, 1, True, False, True)
        shared(s_d, d_rows, 0)
        add_d(0, 1, False)
        forward(1)
        forward(2)
        ring(3)
        shared(s_f, f_rows, 0)
        add_ef(0, 1, False, True, False)
        own.append(activate(0))
        ringed(1)
        shared(s_d, d_rows, 1, 2)
        add_d(1, 2, True)
        ringed(2)
        shared(s_f, f_rows, 1, 2)
        add_ef(1, 2, True, True, False)
        own.append(activate(1, 2))
        ringed(3)
        shared(s_d, d_rows, 3)
        add_d(3, 1, True)
        wd_wait()
        project_e(1, 2)
        shared(s_f, f_rows, 3)
        add_ef(3, 1, True, True, False)
        own.append(activate(3))
        ring_back(1)
        ring_back(2)
        project_e(3)
        project_e(0)
        ringed_back(1)
        ringed_back(2)
        ring_back(0)
        ringed_back(3)
        ringed_back(0)
        for j in range(3):
            copies.arrived(s_bz + j, e_zin.at[j])
        e_sum[z % 2] = total_of(e_part[0, 0], e_zin[2])
        e_sum[1 - z % 2] = total_of(e_zin[0], e_zin[1])
        join_pairs(e_sum, e_back)
        s_x = copies.take(3)
        own += x_return(s_x, e_back, e_end)
        x_returned(s_x, e_end)
        last[...] = (hid[...] + weighted(e_end[...].reshape(slots, half))).astype(BF16)
        pltpu.make_async_copy(last, o_ref.at[:, mine], load_sems.at[0]).start()
        own.append(copies.send(s_last, last, o_ref.at[:, mine], other))
        for copy in own:
            copy.wait_send()

    def core_one():
        own = []
        eye = diagonal.astype(BF16)
        over_slots = (((1,), (1,)), ((), ()))
        for i, lanes in enumerate((coarse, fine)):
            lanes = lax.dot_general(eye, lanes, over_slots, preferred_element_type=F32)
            d_raw[0, 0, :, WIDE + i * slots : WIDE + (i + 1) * slots] = lanes.astype(BF16)
        d_raw[0, 0, :, 0:WIDE] = normed[:, 0:WIDE]
        s_dy, s_dz = copies.take(3), copies.take(12)
        for i in range(3):
            own.append(copies.send(s_dy + i, d_raw.at[0, 0], d_raw.at[0, i + 1], y_to[i]))

        def raw_to_z(ky, targets):
            for i in targets:
                own.append(
                    copies.send(
                        s_dz + 3 * ky + i, d_raw.at[0, ky], d_raw.at[i + 1, ky], z_to[i]
                    )
                )

        raw_to_z(0, (0, 1))
        outgoing = place_slots(normed[:, WIDE:])
        for i in range(4):
            f_first[i] = outgoing[i * rows : (i + 1) * rows]
        s_x = copies.take(3)
        own += x_send(s_x, f_first, f_x)
        own += share_wd()
        for ky in (1, 2, 3):
            copies.arrived(s_dy + ky - 1, d_raw.at[0, ky])
            raw_to_z(ky, (0, 1))

        group_slots = 4 * 4 * CAP
        slot_in = lax.broadcasted_iota(jnp.int32, (slots, group_slots), 0)
        slot_at = lax.broadcasted_iota(jnp.int32, (slots, group_slots), 1)
        wanted = slot_at // (4 * CAP) * (2 * CAP) + zl * CAP + slot_at % CAP
        choose = (slot_in == wanted).astype(BF16)
        row_y = lax.broadcasted_iota(jnp.int32, (4 * rows, group_slots), 0) // rows
        slot_y = lax.broadcasted_iota(jnp.int32, (4 * rows, group_slots), 1) // CAP % 4
        same_y = row_y == slot_y
        s_dx = copies.take(12)

        def select(kz):
            if kz > 0:
                for ky in range(4):
                    copies.arrived(s_dz + 3 * ky + kz - 1, d_raw.at[kz, ky])
            for i in range(2):
                lanes = d_raw[kz, :, :, WIDE + i * slots : WIDE + (i + 1) * slots]
                lanes = jnp.dot(
                    lanes.reshape(4 * rows, slots), choose, preferred_element_type=F32
                )
                d_weights[kz, i] = jnp.where(same_y, lanes, 0.0).astype(BF16)
            chosen = (d_weights[kz, 0].astype(F32) > 0.0).astype(BF16)
            data = d_raw[kz, :, :, 0:WIDE].reshape(4 * rows, WIDE)
            value = lax.dot_general(chosen, data, over_rows, preferred_element_type=F32)
            d_slots[kz] = value.astype(BF16).reshape(4, 4 * CAP, WIDE)
            for i in range(3):
                own.append(
                    copies.send(
                        s_dx + 3 * kz + i, d_slots.at[kz, x_out[i]], d_rows.at[kz, i + 1], x_to[i]
                    )
                )
            d_rows[kz, 0] = d_slots[kz, x]

        def placed(kz):
            for i in range(3):
                copies.arrived(s_dx + 3 * kz + i, d_rows.at[kz, i + 1])
            own.append(share(s_d, d_rows, kz))

        select(0)
        for i in range(3):
            copies.arrived(s_x + i, f_x.at[i + 1])
        split_pairs(f_x, f_z)
        s_up, s_down = copies.take(), copies.take()
        own.append(copies.send(s_up, f_z, f_y.at[0], y_up))
        own.append(copies.send(s_down, f_z, f_y.at[1], y_down))
        s_z = copies.take(12)

        def spread(ky, block, targets):
            for j in targets:
                own.append(
                    copies.send(
                        s_z + 3 * ky + j, block.at[z_out[j] % 2], f_rows.at[j + 1, ky], z_to[j]
                    )
                )

        def gathered(kz):
            for ky in range(4):
                if kz > 0:
                    copies.arrived(s_z + 3 * ky + kz - 1, f_rows.at[kz, ky])
            own.append(share(s_f, f_rows, kz))

        s_bdx, s_bz, s_bdz = copies.take(12), copies.take(3), copies.take(3)

        def project_df(k, count=1):
            inner_wait(k, count)

            def put_d(n, value):
                columns = pl.ds(pl.multiple_of(n * 1024, 1024), 1024)
                for i in range(count):
                    for kx in range(4):
                        for ky in (0, 2):
                            at = i * 128 + ky * 32 + kx * CAP
                            pair = [value[at : at + CAP], value[at + 32 : at + 32 + CAP]]
                            d_part[k + i, kx, ky * CAP : (ky + 2) * CAP, columns] = (
                                jnp.concatenate(pair, axis=0).astype(BF16)
                            )

            def put_f(n, value):
                f_part[k : k + count] = value.astype(BF16).reshape(count, 4, 32, half - WIDE)

            project(k, count, 0, WIDE, put_d)
            for j in range(k, k + count):
                for i in range(3):
                    own.append(
                        copies.send(
                            s_bdx + 3 * j + i,
                            d_part.at[j, i + 1],
                            d_xin.at[j, x],
                            x_to[home[i]],
                        )
                    )
                d_xin[j, x] = d_part[j, 0]
            project(k, count, WIDE, half, put_f)
            for j in range(k, k + count):
                if j > 0:
                    i = j - 1
                    own.append(copies.send(s_bz + i, f_part.at[j], f_zin.at[i], z_to[home[i]]))

        def combine(kz):
            for i, d in enumerate((1, -1, 2)):
                copies.arrived(s_bdx + 3 * kz + i, d_xin.at[kz, shift(x, d)])
            data = d_xin[kz].reshape(group_slots, WIDE)
            value = jnp.dot(d_weights[kz, 0], data, preferred_element_type=F32)
            value += jnp.dot(d_weights[kz, 1], data, preferred_element_type=F32)
            d_group[kz] = value.astype(BF16)
            if kz > 0:
                i = kz - 1
                own.append(copies.send(s_bdz + i, d_group.at[kz], d_zin.at[i], z_to[home[i]]))

        select(1)
        select(2)
        s_up2, s_down2 = copies.take(), copies.take()
        copies.arrived(s_up, f_y.at[0])
        own.append(copies.send(s_up2, f_y.at[0, 0], f_y.at[2, 0], y_up))
        copies.arrived(s_down, f_y.at[1])
        own.append(copies.send(s_down2, f_y.at[1, 1], f_y.at[2, 1], y_down))
        pl.semaphore_wait(turn, 1)
        for ky in range(4):
            raw_to_z(ky, (2,))
        spread(0, f_z, (0, 1))
        spread(1, f_y.at[0], (0, 1))
        spread(2, f_y.at[1], (0, 1))
        f_rows[0, 0] = f_z[z % 2]
        f_rows[0, 1] = f_y[0, z % 2]
        f_rows[0, 2] = f_y[1, z % 2]
        placed(0)
        copies.arrived(s_up2, f_y.at[2, 0])
        copies.arrived(s_down2, f_y.at[2, 1])
        spread(3, f_y.at[2], (0, 1))
        f_rows[0, 3] = f_y[2, z % 2]
        gathered(0)
        for ky, block in enumerate((f_z, f_y.at[0], f_y.at[1], f_y.at[2])):
            spread(ky, block, (2,))
        load_wait()
        add_d(0, 1, True)
        shared(s_e, e_rows, 0)
        add_ef(0, 1, True, True, False)
        own.append(activate(0))
        select(3)
        placed(1)
        placed(2)
        gathered(1)
        gathered(2)
        add_d(1, 2, True)
        placed(3)
        gathered(3)
        shared(s_e, e_rows, 1, 2)
        add_ef(1, 2, True, True, False)
        own.append(activate(1, 2))
        add_d(3, 1, True)
        wd_wait()
        project_df(1, 2)
        shared(s_e, e_rows, 3)
        add_ef(3, 1, True, True, False)
        own.append(activate(3))
        project_df(3)
        project_df(0)
        combine(1)
        combine(2)
        for i in range(3):
            copies.arrived(s_bz + i, f_zin.at[i])
        s_bup, s_bdown = copies.take(), copies.take()
        s_bup2, s_bdown2 = copies.take(), copies.take()
        for ky in (3, 2, 1, 0):
            f_sum[ky, z % 2] = total_of(f_part[0, ky], f_zin[2, ky])
            f_sum[ky, 1 - z % 2] = total_of(f_zin[0, ky], f_zin[1, ky])
            if ky == 3:
                own.append(copies.send(s_bup, f_sum.at[3, 0], f_up, y_up))
                own.append(copies.send(s_bdown, f_sum.at[3, 1], f_down, y_down))
        combine(3)
        combine(0)
        copies.arrived(s_bup, f_up)
        f_sum[2, 0] = total_of(f_sum[2, 0], f_up[...])
        own.append(copies.send(s_bup2, f_sum.at[2], f_up2, y_up))
        copies.arrived(s_bdown, f_down)
        f_sum[1, 1] = total_of(f_sum[1, 1], f_down[...])
        own.append(copies.send(s_bdown2, f_sum.at[1], f_down2, y_down))
        for i in range(3):
            copies.arrived(s_bdz + i, d_zin.at[i])
        value = total_of(d_group[0], d_zin[0], d_zin[1], d_zin[2])
        d_sum[...] = value.reshape(4, rows, WIDE)
        s_dy = copies.take(3)
        for i in range(3):
            own.append(copies.send(s_dy + i, d_sum.at[i + 1], d_yin.at[i], y_to[home[i]]))
        copies.arrived(s_bup2, f_up2)
        copies.arrived(s_bdown2, f_down2)
        f_sum[0] = total_of(f_sum[0], f_up2[...], f_down2[...])
        join_pairs(f_sum.at[0], f_back)
        s_x = copies.take(3)
        own += x_return(s_x, f_back, f_end)
        x_returned(s_x, f_end)
        value = hid[:, WIDE:] + weighted(f_end[...].reshape(slots, half - WIDE))
        last[:, WIDE:] = value.astype(BF16)
        value = hid[:, 0:WIDE] + d_sum[0].astype(F32)
        for i in range(3):
            copies.arrived(s_dy + i, d_yin.at[i])
            value = value + d_yin[i].astype(F32)
        last[:, 0:WIDE] = value.astype(BF16)
        pltpu.make_async_copy(last, o_ref.at[:, mine], load_sems.at[0]).start()
        own.append(copies.send(s_last, last, o_ref.at[:, mine], other))
        for copy in own:
            copy.wait_send()

    common = copies.used
    pl.when(c == 0)(core_zero)
    used_zero, copies.used = copies.used, common
    pl.when(c == 1)(core_one)
    assert max(used_zero, copies.used) <= SEMS

    copies.arrived(s_last, o_ref.at[:, theirs])
    pltpu.make_async_copy(last, o_ref.at[:, mine], load_sems.at[0]).wait()
    for copy in sent:
        copy.wait_send()


def on_device(
    queries,
    new_keys,
    new_values,
    fork_map,
    key_cache,
    value_cache,
    cache_lengths,
    residual,
    norm_gain,
    expert_ids,
    gate_weights,
    w_gate,
    w_up,
    w_down,
):
    rows, width = residual.shape
    half = width // 2
    narrow = half - WIDE
    hidden = w_gate.shape[2]
    prompts, cache_len, kv_width = key_cache.shape
    heads = kv_width // HD
    vmem = pl.BlockSpec(memory_space=VMEM)
    hbm = pl.BlockSpec(memory_space=pl.ANY)
    return pl.pallas_call(
        layer_kernel,
        out_shape=jax.ShapeDtypeStruct((rows, width), BF16),
        in_specs=[pl.BlockSpec(memory_space=pltpu.SMEM)] + [vmem] * 4 + [hbm] * 9,
        out_specs=hbm,
        scratch_shapes=[
            VMEM((rows, half), BF16),
            VMEM((rows, kv_width), BF16),
            VMEM((rows, kv_width), BF16),
            VMEM((heads, prompts, cache_len, HD), BF16),
            VMEM((heads, prompts, cache_len, HD), BF16),
            VMEM((rows, half), BF16),
            VMEM((width, hidden), BF16),
            VMEM((width, hidden), BF16),
            VMEM((2 * hidden, half), BF16),
            VMEM((2, rows, HD), F32),
            VMEM((rows, half), F32),
            VMEM((512, hidden), F32),
            VMEM((512, hidden), F32),
            VMEM((2, 512, hidden), BF16),
            VMEM((rows, half), BF16),
            VMEM((4, 16, half), BF16),
            VMEM((4, 16, half), BF16),
            VMEM((2, 32, half), BF16),
            VMEM((4, 4, 32, half), BF16),
            VMEM((4, 4, 32, half), BF16),
            VMEM((4, 16, half), BF16),
            VMEM((4, 16, half), BF16),
            VMEM((4, 32, half), BF16),
            VMEM((4, 32, half), BF16),
            VMEM((3, 32, half), BF16),
            VMEM((2, 32, half), BF16),
            VMEM((4, 16, half), BF16),
            VMEM((4, 16, half), BF16),
            VMEM((4, 16, narrow), BF16),
            VMEM((4, 16, narrow), BF16),
            VMEM((2, 32, narrow), BF16),
            VMEM((3, 2, 32, narrow), BF16),
            VMEM((4, 4, 32, narrow), BF16),
            VMEM((4, 4, 32, narrow), BF16),
            VMEM((3, 4, 32, narrow), BF16),
            VMEM((4, 2, 32, narrow), BF16),
            VMEM((32, narrow), BF16),
            VMEM((32, narrow), BF16),
            VMEM((2, 32, narrow), BF16),
            VMEM((2, 32, narrow), BF16),
            VMEM((4, 16, narrow), BF16),
            VMEM((4, 16, narrow), BF16),
            VMEM((4, 4, rows, WIDE + HD), BF16),
            VMEM((4, 2, 4 * rows, HD), BF16),
            VMEM((4, 4, 32, WIDE), BF16),
            VMEM((4, 4, 32, WIDE), BF16),
            VMEM((4, 4, 32, WIDE), BF16),
            VMEM((4, 4, 32, WIDE), BF16),
            VMEM((4, 4 * rows, WIDE), BF16),
            VMEM((3, 4 * rows, WIDE), BF16),
            VMEM((4, rows, WIDE), BF16),
            VMEM((3, rows, WIDE), BF16),
            pltpu.SemaphoreType.DMA((SEMS,)),
            pltpu.SemaphoreType.DMA((SEMS,)),
            pltpu.SemaphoreType.DMA((7 + 2 * heads,)),
            pltpu.SemaphoreType.REGULAR,
        ],
        compiler_params=pltpu.CompilerParams(
            collective_id=0, has_side_effects=True, vmem_limit_bytes=60 * 2**20
        ),
    )(
        cache_lengths,
        fork_map.reshape(1, rows),
        norm_gain.reshape(width // HD, HD),
        expert_ids.T,
        gate_weights.T,
        queries,
        new_keys,
        new_values,
        key_cache,
        value_cache,
        residual,
        w_gate[0],
        w_up[0],
        w_down[0],
    )


def solution(mesh):
    in_specs = (
        P(("grp", "shard"), "pool"),
        P(("grp", "shard"), "pool"),
        P(("grp", "shard"), "pool"),
        P(("grp", "shard")),
        P(("grp", "shard"), None, "pool"),
        P(("grp", "shard"), None, "pool"),
        P(("grp", "shard")),
        P(("grp", "shard"), None),
        P(),
        P(("grp", "shard"), None),
        P(("grp", "shard"), None),
        P("grp", None, ("pool", "shard")),
        P("grp", None, ("pool", "shard")),
        P("grp", ("pool", "shard"), None),
    )
    out_specs = P(("grp", "shard"), None)
    return jax.shard_map(
        on_device, mesh=mesh, in_specs=in_specs, out_specs=out_specs, check_vma=False
    )
```

```python
import math

import jax
import jax.numpy as jnp
from jax import lax
from jax.experimental import pallas as pl
from jax.experimental.pallas import tpu as pltpu
from jax.sharding import PartitionSpec as P

HD = 128
CAP = 8
MESH = pl.DeviceIdType.MESH
F32 = jnp.float32
BF16 = jnp.bfloat16
VMEM = pltpu.VMEM


def landed(ref, sem):
    pltpu.make_async_copy(ref, ref, sem).wait()


class Copies:
    def __init__(self, send_sems, recv_sems):
        self.send_sems, self.recv_sems, self.used = send_sems, recv_sems, 0

    def take(self, count=1):
        first = self.used
        self.used += count
        return first

    def send(self, index, src, dst, device):
        copy = pltpu.make_async_remote_copy(
            src_ref=src,
            dst_ref=dst,
            send_sem=self.send_sems.at[index],
            recv_sem=self.recv_sems.at[index],
            device_id=device,
            device_id_type=MESH,
        )
        copy.start()
        return copy

    def arrived(self, index, ref):
        landed(ref, self.recv_sems.at[index])


SEMS = 112
WIDE = 2048


def layer_kernel(
    lens_ref,
    fork_ref,
    gain_ref,
    ids_ref,
    gw_ref,
    q_hbm,
    nk_hbm,
    nv_hbm,
    k_hbm,
    v_hbm,
    res_hbm,
    wg_hbm,
    wu_hbm,
    wd_hbm,
    o_ref,
    q_in,
    nk_in,
    nv_in,
    k_in,
    v_in,
    res_in,
    wg,
    wu,
    wd,
    ssq,
    hid,
    gate,
    up,
    inner,
    last,
    e_first,
    e_x,
    e_z,
    e_rows,
    e_part,
    e_up,
    e_down,
    e_up2,
    e_down2,
    e_zin,
    e_sum,
    e_back,
    e_end,
    f_first,
    f_x,
    f_z,
    f_y,
    f_rows,
    f_part,
    f_zin,
    f_sum,
    f_up,
    f_down,
    f_up2,
    f_down2,
    f_back,
    f_end,
    d_raw,
    d_weights,
    d_slots,
    d_rows,
    d_part,
    d_xin,
    d_group,
    d_zin,
    d_sum,
    d_yin,
    send_sems,
    recv_sems,
    load_sems,
    turn,
):
    c = lax.axis_index("pool")
    grp = lax.axis_index("grp")
    shard = lax.axis_index("shard")
    x, zl = grp // 2, grp % 2
    y, zh = shard // 2, shard % 2
    z = zh * 2 + zl
    rows, width = o_ref.shape
    half = width // 2
    hidden = wg.shape[1]

    def device(px, py, pz, pc=c):
        return (pc, px * 2 + pz % 2, py * 2 + pz // 2)

    def shift(a, d):
        return (a + d + 4) % 4

    other = device(x, y, z, 1 - c)
    x_out, y_out, z_out = ([shift(a, d) for d in (1, -1, 2)] for a in (x, y, z))
    x_to = [device(t, y, z) for t in x_out]
    y_to = [device(x, t, z) for t in y_out]
    z_to = [device(x, y, t) for t in z_out]
    y_up, y_down = y_to[:2]
    home = (1, 0, 2)
    mine = pl.ds(pl.multiple_of(c * half, half), half)
    theirs = pl.ds(pl.multiple_of((1 - c) * half, half), half)
    mine_hidden = pl.ds(pl.multiple_of(c * hidden, hidden), hidden)

    def load(index, src, dst):
        copy = pltpu.make_async_copy(src, dst, load_sems.at[index])
        copy.start()
        return copy

    heads = k_in.shape[0]
    group = half // (heads * HD)
    query_loads = [load(0, q_hbm, q_in), load(1, nk_hbm, nk_in), load(2, nv_hbm, nv_in)]
    cache_loads = []
    for head in range(heads):
        columns = slice(head * HD, (head + 1) * HD)
        cache_loads.append(
            (
                load(3 + 2 * head, k_hbm.at[:, :, columns], k_in.at[head]),
                load(4 + 2 * head, v_hbm.at[:, :, columns], v_in.at[head]),
            )
        )
    res_load = load(3 + 2 * heads, res_hbm.at[:, mine], res_in)
    barrier = pltpu.get_barrier_semaphore()
    partners = [other] + x_to + y_to + z_to
    for partner in partners:
        pl.semaphore_signal(barrier, inc=1, device_id=partner, device_id_type=MESH)

    prompts, cache_len = k_in.shape[1], k_in.shape[2]
    diagonal = lax.broadcasted_iota(jnp.int32, (rows, rows), 0) == lax.broadcasted_iota(
        jnp.int32, (rows, rows), 1
    )
    prompt = jnp.sum(jnp.where(diagonal, fork_ref[...] % prompts, 0), axis=1, keepdims=True)
    prompt = jnp.concatenate([prompt] * group, axis=0)
    place = lax.broadcasted_iota(jnp.int32, (rows * group, cache_len), 1)
    limits = [jnp.where(prompt == p, lens_ref[p], 0) for p in range(prompts)]
    power = HD ** (-0.5) * math.log2(math.e)
    for query_load in query_loads:
        query_load.wait()
    attended = []
    for head in range(heads):
        at = head * group * HD
        queries = jnp.concatenate(
            [q_in[:, at + i * HD : at + (i + 1) * HD] for i in range(group)], axis=0
        )
        new_key = nk_in[:, head * HD : (head + 1) * HD].astype(F32)
        new_value = nv_in[:, head * HD : (head + 1) * HD].astype(F32)
        own = queries.astype(F32) * jnp.concatenate([new_key] * group, axis=0)
        own = jnp.sum(own, axis=1, keepdims=True)
        top = own
        scores = []
        cache_loads[head][0].wait()
        for p in range(prompts):
            score = lax.dot_general(
                queries, k_in[head, p], (((1,), (1,)), ((), ())), preferred_element_type=F32
            )
            score = jnp.where(place < limits[p], score, -1e30)
            scores.append(score)
            top = jnp.maximum(top, jnp.max(score, axis=1, keepdims=True))
        own_weight = jnp.exp2((own - top) * power)
        total = own_weight
        mixed = own_weight * jnp.concatenate([new_value] * group, axis=0)
        cache_loads[head][1].wait()
        for p in range(prompts):
            raw = jnp.exp2((scores[p] - top) * power)
            total = total + jnp.sum(raw, axis=1, keepdims=True)
            mixed = mixed + jnp.dot(
                raw.astype(BF16), v_in[head, p], preferred_element_type=F32
            )
        out = (mixed / total).astype(BF16).astype(F32)
        attended += [out[i * rows : (i + 1) * rows] for i in range(group)]
    attended = jnp.concatenate(attended, axis=1)
    loads = [
        load(4 + 2 * heads, wg_hbm, wg),
        load(5 + 2 * heads, wu_hbm, wu),
        load(6 + 2 * heads, wd_hbm.at[:, mine], wd.at[mine_hidden]),
    ]

    slots = 4 * rows
    slot = lax.broadcasted_iota(jnp.int32, (slots, rows), 0)
    pick_a = (ids_ref[0:1] == slot // CAP).astype(F32)
    pick_b = (ids_ref[1:2] == slot // CAP).astype(F32)
    before = (
        lax.broadcasted_iota(jnp.int32, (rows, rows), 0)
        < lax.broadcasted_iota(jnp.int32, (rows, rows), 1)
    ).astype(F32)
    rank = jnp.dot(pick_a + pick_b, before, preferred_element_type=F32)
    here = (rank == (slot % CAP).astype(F32)).astype(F32)
    placing = ((pick_a + pick_b) * here).astype(BF16)
    weighting = (pick_a * gw_ref[0:1] + pick_b * gw_ref[1:2]) * here
    coarse = weighting.astype(BF16)
    fine = (weighting - coarse.astype(F32)).astype(BF16)
    gain = gain_ref[...].astype(F32)
    gain_rows = half // HD
    gain = jnp.where(c == 0, gain[:gain_rows], gain[gain_rows:])

    pl.semaphore_wait(barrier, len(partners))

    copies = Copies(send_sems, recv_sems)
    sent = []

    res_load.wait()
    hidden_state = res_in[...].astype(F32) + attended
    hid[...] = hidden_state
    square = jnp.sum(hidden_state * hidden_state, axis=1, keepdims=True)
    ssq[0] = jnp.broadcast_to(square, (rows, HD))
    s_ssq = copies.take()
    sent.append(copies.send(s_ssq, ssq.at[0], ssq.at[1], other))

    copies.arrived(s_ssq, ssq.at[1])
    meansq = (ssq[0][:, 0:1] + ssq[1][:, 0:1]) / width
    normed = hidden_state * lax.rsqrt(meansq + 1e-05)
    normed = jnp.concatenate(
        [normed[:, i * HD : (i + 1) * HD] * gain[i : i + 1] for i in range(gain_rows)], axis=1
    ).astype(BF16)
    over_rows = (((0,), (0,)), ((), ()))
    s_e, s_f, s_d = copies.take(4), copies.take(4), copies.take(4)
    s_near = copies.take(4)
    s_inner = copies.take(4)
    s_last = copies.take()
    s_wd = copies.take()

    def split_pairs(src, dst):
        for part_z in range(2):
            for pair in range(2):
                a = src[2 * pair].astype(F32)[part_z * CAP : (part_z + 1) * CAP]
                b = src[2 * pair + 1].astype(F32)[part_z * CAP : (part_z + 1) * CAP]
                dst[part_z, pair * 16 : (pair + 1) * 16] = jnp.concatenate([a, b], axis=0).astype(
                    BF16
                )

    def join_pairs(src, dst):
        for pair in range(2):
            a = src[0, pair * 16 : (pair + 1) * 16].astype(F32)
            b = src[1, pair * 16 : (pair + 1) * 16].astype(F32)
            dst[2 * pair] = jnp.concatenate([a[:CAP], b[:CAP]], axis=0).astype(BF16)
            dst[2 * pair + 1] = jnp.concatenate([a[CAP:], b[CAP:]], axis=0).astype(BF16)

    def dots(parts, put, step):
        for weight, total in ((wg, gate), (wu, up)):

            @pl.loop(0, hidden // step)
            def _(n):
                columns = pl.ds(pl.multiple_of(n * step, step), step)
                value = None
                for data, weight_rows in parts:
                    term = jnp.dot(data, weight[weight_rows, columns], preferred_element_type=F32)
                    value = term if value is None else value + term
                put(total, columns, value)

    def e_of(k, count):
        return e_rows[k : k + count].reshape(count * 128, half), slice(0, half)

    def f_of(k, count):
        data = f_rows[k : k + count].reshape(count * 128, half - WIDE)
        return data, slice(half + WIDE, width)

    def add_ef(k, count, use_e, use_f, write):
        at = slice(k * 128, (k + count) * 128)
        parts = [e_of(k, count)] * use_e + [f_of(k, count)] * use_f

        def put(total, columns, value):
            if write:
                total[at, columns] = value
            else:
                total[at, columns] += value

        dots(parts, put, 256)

    def add_d(k, count, write):
        def put(total, columns, value):
            for i in range(count * 16):
                kz, kx, ky = k + i // 16, i // 4 % 4, i % 4
                at = kz * 128 + ky * 32 + kx * CAP
                rows_here = value[i * CAP : (i + 1) * CAP]
                if write:
                    total[at : at + CAP, columns] = rows_here
                else:
                    total[at : at + CAP, columns] += rows_here

        data = d_rows[k : k + count].reshape(count * 128, WIDE)
        dots([(data, slice(half, half + WIDE))], put, 256)

    def share(first, ref, k):
        return copies.send(first + k, ref.at[k], ref.at[k], other)

    def shared(first, ref, k, count=1):
        for i in range(k, k + count):
            copies.arrived(first + i, ref.at[i])

    def shared_e(k, count=1):
        for i in range(k, k + count):
            copies.arrived(s_near + i, e_rows.at[i, 0:3])
            copies.arrived(s_e + i, e_rows.at[i, 3])

    def share_wd():
        src = wd_hbm.at[:, theirs]
        return [copies.send(s_wd, src, wd.at[mine_hidden], other)]

    def wd_wait():
        loads[2].wait()
        at = pl.multiple_of((1 - c) * hidden, hidden)
        copies.arrived(s_wd, wd.at[pl.ds(at, hidden)])

    def load_wait():
        for load in loads[:2]:
            load.wait()

    def activate(k, count=1):
        at = slice(k * 128, (k + count) * 128)
        value = gate[at]
        inner[c, at] = (value / (1.0 + jnp.exp(-value)) * up[at]).astype(BF16)
        return copies.send(s_inner + k, inner.at[c, at], inner.at[c, at], other)

    def inner_wait(k, count=1):
        at = slice(k * 128, (k + count) * 128)
        copies.arrived(s_inner + k, inner.at[1 - c, at])

    def project(k, count, start, stop, put):
        at = slice(k * 128, (k + count) * 128)

        @pl.loop(0, (stop - start) // 1024)
        def _(n):
            columns = pl.ds(pl.multiple_of(start + n * 1024, 1024), 1024)
            value = jnp.dot(inner[0, at], wd[0:hidden, columns], preferred_element_type=F32)
            value += jnp.dot(
                inner[1, at], wd[hidden : 2 * hidden, columns], preferred_element_type=F32
            )
            put(n, value)

    def total_of(*refs):
        value = refs[0].astype(F32)
        for ref in refs[1:]:
            value = value + ref.astype(F32)
        return value.astype(BF16)

    def x_send(first, src, dst):
        done = []
        for i in range(3):
            done.append(copies.send(first + i, src.at[x_out[i]], dst.at[i + 1], x_to[i]))
        dst[0] = src[x]
        return done

    def x_return(first, src, dst):
        done = []
        for i in range(3):
            done.append(copies.send(first + i, src.at[i + 1], dst.at[x], x_to[home[i]]))
        dst[x] = src[0]
        return done

    def x_returned(first, dst):
        for i, d in enumerate((1, -1, 2)):
            copies.arrived(first + i, dst.at[shift(x, d)])

    def weighted(data):
        value = lax.dot_general(coarse, data, over_rows, preferred_element_type=F32)
        return value + lax.dot_general(fine, data, over_rows, preferred_element_type=F32)

    def place_slots(columns):
        return jnp.dot(placing, columns, preferred_element_type=F32).astype(BF16)

    def core_zero():
        own = []
        outgoing = place_slots(normed)
        for i in range(4):
            e_first[i] = outgoing[i * rows : (i + 1) * rows]
        s_x = copies.take(3)
        own += x_send(s_x, e_first, e_x)
        own += share_wd()
        for i in range(3):
            copies.arrived(s_x + i, e_x.at[i + 1])
        split_pairs(e_x, e_z)
        s_z = copies.take(3)

        def to_z(k):
            return copies.send(s_z + k, e_z.at[z_out[k] % 2], e_rows.at[k + 1, 0], z_to[k])

        first_z = [to_z(0), to_z(1)]
        e_rows[0, 0] = e_z[z % 2]
        straight, straight_back = (0, 3), (0, 1, 2, 3)
        s_up, s_down, s_up2, s_down2 = (copies.take(4) for _ in range(4))

        def ring(j):
            if j > 0:
                copies.arrived(s_z + j - 1, e_rows.at[j, 0])
            own.append(copies.send(s_up + j, e_rows.at[j, 0], e_rows.at[j, 1], y_up))
            own.append(copies.send(s_down + j, e_rows.at[j, 0], e_rows.at[j, 2], y_down))
            if j in straight:
                own.append(copies.send(s_up2 + j, e_rows.at[j, 0], e_rows.at[j, 3], y_to[2]))

        def share_near(j):
            near = e_rows.at[j, 0:3]
            return copies.send(s_near + j, near, near, other)

        def forward(j):
            if j in straight:
                return
            copies.arrived(s_up + j, e_rows.at[j, 1])
            own.append(
                copies.send(s_up2 + j, e_rows.at[j, 1, 0:16], e_rows.at[j, 3, 0:16], y_up)
            )
            copies.arrived(s_down + j, e_rows.at[j, 2])
            own.append(
                copies.send(s_down2 + j, e_rows.at[j, 2, 16:32], e_rows.at[j, 3, 16:32], y_down)
            )
            own.append(share_near(j))

        def ringed(j):
            if j in straight:
                copies.arrived(s_up + j, e_rows.at[j, 1])
                copies.arrived(s_down + j, e_rows.at[j, 2])
                own.append(share_near(j))
                copies.arrived(s_up2 + j, e_rows.at[j, 3])
            else:
                copies.arrived(s_up2 + j, e_rows.at[j, 3, 0:16])
                copies.arrived(s_down2 + j, e_rows.at[j, 3, 16:32])
            far = e_rows.at[j, 3]
            own.append(copies.send(s_e + j, far, far, other))

        s_bup, s_bdown, s_bup2, s_bdown2 = (copies.take(4) for _ in range(4))
        s_bz = copies.take(3)

        def project_e(k, count=1):
            inner_wait(k, count)

            def put(n, value):
                columns = pl.ds(pl.multiple_of(n * 1024, 1024), 1024)
                value = value.astype(BF16).reshape(count, 4, 32, 1024)
                e_part[k : k + count, :, :, columns] = value

            project(k, count, 0, half, put)
            for j in range(k, k + count):
                far_up, far_down = (y_to[2], y_to[2]) if j in straight_back else (y_up, y_down)
                own.append(copies.send(s_bup + j, e_part.at[j, 3, 0:16], e_up.at[j], far_up))
                own.append(
                    copies.send(s_bdown + j, e_part.at[j, 3, 16:32], e_down.at[j], far_down)
                )
                if j in straight_back:
                    own.append(copies.send(s_bup2 + j, e_part.at[j, 2], e_up2.at[j], y_up))
                    own.append(copies.send(s_bdown2 + j, e_part.at[j, 1], e_down2.at[j], y_down))

        def ring_back(j):
            if j in straight_back:
                return
            copies.arrived(s_bup + j, e_up.at[j])
            e_part[j, 2, 0:16] = total_of(e_part[j, 2, 0:16], e_up[j])
            own.append(copies.send(s_bup2 + j, e_part.at[j, 2], e_up2.at[j], y_up))
            copies.arrived(s_bdown + j, e_down.at[j])
            e_part[j, 1, 16:32] = total_of(e_part[j, 1, 16:32], e_down[j])
            own.append(copies.send(s_bdown2 + j, e_part.at[j, 1], e_down2.at[j], y_down))

        def ringed_back(j):
            copies.arrived(s_bup2 + j, e_up2.at[j])
            copies.arrived(s_bdown2 + j, e_down2.at[j])
            if j in straight_back:
                copies.arrived(s_bup + j, e_up.at[j])
                copies.arrived(s_bdown + j, e_down.at[j])
                e_part[j, 0, 0:16] = total_of(
                    e_part[j, 0, 0:16], e_up2[j, 0:16], e_down2[j, 0:16], e_up[j]
                )
                e_part[j, 0, 16:32] = total_of(
                    e_part[j, 0, 16:32], e_up2[j, 16:32], e_down2[j, 16:32], e_down[j]
                )
            else:
                e_part[j, 0] = total_of(e_part[j, 0], e_up2[j], e_down2[j])
            if j > 0:
                i = j - 1
                own.append(copies.send(s_bz + i, e_part.at[j, 0], e_zin.at[i], z_to[home[i]]))

        ring(0)
        for copy in first_z:
            copy.wait_send()
        last_z = to_z(2)
        forward(0)
        last_z.wait_send()
        pl.semaphore_signal(turn, inc=1, device_id=other, device_id_type=MESH)
        ring(1)
        ring(2)
        ringed(0)
        load_wait()
        add_ef(0, 1, True, False, True)
        shared(s_d, d_rows, 0)
        add_d(0, 1, False)
        forward(1)
        forward(2)
        ring(3)
        shared(s_f, f_rows, 0)
        add_ef(0, 1, False, True, False)
        own.append(activate(0))
        ringed(1)
        shared(s_d, d_rows, 1, 2)
        add_d(1, 2, True)
        ringed(2)
        shared(s_f, f_rows, 1, 2)
        add_ef(1, 2, True, True, False)
        own.append(activate(1, 2))
        ringed(3)
        shared(s_d, d_rows, 3)
        add_d(3, 1, True)
        wd_wait()
        project_e(1, 2)
        shared(s_f, f_rows, 3)
        add_ef(3, 1, True, True, False)
        own.append(activate(3))
        ring_back(1)
        ring_back(2)
        project_e(3)
        project_e(0)
        ringed_back(1)
        ringed_back(2)
        ring_back(0)
        ringed_back(3)
        ringed_back(0)
        for j in range(3):
            copies.arrived(s_bz + j, e_zin.at[j])
        e_sum[z % 2] = total_of(e_part[0, 0], e_zin[2])
        e_sum[1 - z % 2] = total_of(e_zin[0], e_zin[1])
        join_pairs(e_sum, e_back)
        s_x = copies.take(3)
        own += x_return(s_x, e_back, e_end)
        x_returned(s_x, e_end)
        last[...] = (hid[...] + weighted(e_end[...].reshape(slots, half))).astype(BF16)
        pltpu.make_async_copy(last, o_ref.at[:, mine], load_sems.at[0]).start()
        own.append(copies.send(s_last, last, o_ref.at[:, mine], other))
        for copy in own:
            copy.wait_send()

    def core_one():
        own = []
        eye = diagonal.astype(BF16)
        over_slots = (((1,), (1,)), ((), ()))
        for i, lanes in enumerate((coarse, fine)):
            lanes = lax.dot_general(eye, lanes, over_slots, preferred_element_type=F32)
            d_raw[0, 0, :, WIDE + i * slots : WIDE + (i + 1) * slots] = lanes.astype(BF16)
        d_raw[0, 0, :, 0:WIDE] = normed[:, 0:WIDE]
        s_dy, s_dz = copies.take(3), copies.take(12)
        for i in range(3):
            own.append(copies.send(s_dy + i, d_raw.at[0, 0], d_raw.at[0, i + 1], y_to[i]))

        def raw_to_z(ky, targets):
            for i in targets:
                own.append(
                    copies.send(
                        s_dz + 3 * ky + i, d_raw.at[0, ky], d_raw.at[i + 1, ky], z_to[i]
                    )
                )

        raw_to_z(0, (0, 1))
        outgoing = place_slots(normed[:, WIDE:])
        for i in range(4):
            f_first[i] = outgoing[i * rows : (i + 1) * rows]
        s_x = copies.take(3)
        own += x_send(s_x, f_first, f_x)
        own += share_wd()
        for ky in (1, 2, 3):
            copies.arrived(s_dy + ky - 1, d_raw.at[0, ky])
            raw_to_z(ky, (0, 1))

        group_slots = 4 * 4 * CAP
        slot_in = lax.broadcasted_iota(jnp.int32, (slots, group_slots), 0)
        slot_at = lax.broadcasted_iota(jnp.int32, (slots, group_slots), 1)
        wanted = slot_at // (4 * CAP) * (2 * CAP) + zl * CAP + slot_at % CAP
        choose = (slot_in == wanted).astype(BF16)
        row_y = lax.broadcasted_iota(jnp.int32, (4 * rows, group_slots), 0) // rows
        slot_y = lax.broadcasted_iota(jnp.int32, (4 * rows, group_slots), 1) // CAP % 4
        same_y = row_y == slot_y
        s_dx = copies.take(12)

        def select(kz):
            if kz > 0:
                for ky in range(4):
                    copies.arrived(s_dz + 3 * ky + kz - 1, d_raw.at[kz, ky])
            for i in range(2):
                lanes = d_raw[kz, :, :, WIDE + i * slots : WIDE + (i + 1) * slots]
                lanes = jnp.dot(
                    lanes.reshape(4 * rows, slots), choose, preferred_element_type=F32
                )
                d_weights[kz, i] = jnp.where(same_y, lanes, 0.0).astype(BF16)
            chosen = (d_weights[kz, 0].astype(F32) > 0.0).astype(BF16)
            data = d_raw[kz, :, :, 0:WIDE].reshape(4 * rows, WIDE)
            value = lax.dot_general(chosen, data, over_rows, preferred_element_type=F32)
            d_slots[kz] = value.astype(BF16).reshape(4, 4 * CAP, WIDE)
            for i in range(3):
                own.append(
                    copies.send(
                        s_dx + 3 * kz + i, d_slots.at[kz, x_out[i]], d_rows.at[kz, i + 1], x_to[i]
                    )
                )
            d_rows[kz, 0] = d_slots[kz, x]

        def placed(kz):
            for i in range(3):
                copies.arrived(s_dx + 3 * kz + i, d_rows.at[kz, i + 1])
            own.append(share(s_d, d_rows, kz))

        select(0)
        for i in range(3):
            copies.arrived(s_x + i, f_x.at[i + 1])
        split_pairs(f_x, f_z)
        s_up, s_down = copies.take(), copies.take()
        own.append(copies.send(s_up, f_z, f_y.at[0], y_up))
        own.append(copies.send(s_down, f_z, f_y.at[1], y_down))
        s_z = copies.take(12)

        def spread(ky, block, targets):
            for j in targets:
                own.append(
                    copies.send(
                        s_z + 3 * ky + j, block.at[z_out[j] % 2], f_rows.at[j + 1, ky], z_to[j]
                    )
                )

        def gathered(kz):
            for ky in range(4):
                if kz > 0:
                    copies.arrived(s_z + 3 * ky + kz - 1, f_rows.at[kz, ky])
            own.append(share(s_f, f_rows, kz))

        s_bdx, s_bz, s_bdz = copies.take(12), copies.take(3), copies.take(3)

        def project_df(k, count=1):
            inner_wait(k, count)

            def put_d(n, value):
                columns = pl.ds(pl.multiple_of(n * 1024, 1024), 1024)
                for i in range(count):
                    for kx in range(4):
                        for ky in (0, 2):
                            at = i * 128 + ky * 32 + kx * CAP
                            pair = [value[at : at + CAP], value[at + 32 : at + 32 + CAP]]
                            d_part[k + i, kx, ky * CAP : (ky + 2) * CAP, columns] = (
                                jnp.concatenate(pair, axis=0).astype(BF16)
                            )

            def put_f(n, value):
                f_part[k : k + count] = value.astype(BF16).reshape(count, 4, 32, half - WIDE)

            project(k, count, 0, WIDE, put_d)
            for j in range(k, k + count):
                for i in range(3):
                    own.append(
                        copies.send(
                            s_bdx + 3 * j + i,
                            d_part.at[j, i + 1],
                            d_xin.at[j, x],
                            x_to[home[i]],
                        )
                    )
                d_xin[j, x] = d_part[j, 0]
            project(k, count, WIDE, half, put_f)
            for j in range(k, k + count):
                if j > 0:
                    i = j - 1
                    own.append(copies.send(s_bz + i, f_part.at[j], f_zin.at[i], z_to[home[i]]))

        def combine(kz):
            for i, d in enumerate((1, -1, 2)):
                copies.arrived(s_bdx + 3 * kz + i, d_xin.at[kz, shift(x, d)])
            data = d_xin[kz].reshape(group_slots, WIDE)
            value = jnp.dot(d_weights[kz, 0], data, preferred_element_type=F32)
            value += jnp.dot(d_weights[kz, 1], data, preferred_element_type=F32)
            d_group[kz] = value.astype(BF16)
            if kz > 0:
                i = kz - 1
                own.append(copies.send(s_bdz + i, d_group.at[kz], d_zin.at[i], z_to[home[i]]))

        select(1)
        select(2)
        s_up2, s_down2 = copies.take(), copies.take()
        copies.arrived(s_up, f_y.at[0])
        own.append(copies.send(s_up2, f_y.at[0, 0], f_y.at[2, 0], y_up))
        copies.arrived(s_down, f_y.at[1])
        own.append(copies.send(s_down2, f_y.at[1, 1], f_y.at[2, 1], y_down))
        pl.semaphore_wait(turn, 1)
        for ky in range(4):
            raw_to_z(ky, (2,))
        spread(0, f_z, (0, 1))
        spread(1, f_y.at[0], (0, 1))
        spread(2, f_y.at[1], (0, 1))
        f_rows[0, 0] = f_z[z % 2]
        f_rows[0, 1] = f_y[0, z % 2]
        f_rows[0, 2] = f_y[1, z % 2]
        placed(0)
        copies.arrived(s_up2, f_y.at[2, 0])
        copies.arrived(s_down2, f_y.at[2, 1])
        spread(3, f_y.at[2], (0, 1))
        f_rows[0, 3] = f_y[2, z % 2]
        gathered(0)
        for ky, block in enumerate((f_z, f_y.at[0], f_y.at[1], f_y.at[2])):
            spread(ky, block, (2,))
        load_wait()
        add_d(0, 1, True)
        shared_e(0)
        add_ef(0, 1, True, True, False)
        own.append(activate(0))
        select(3)
        placed(1)
        placed(2)
        gathered(1)
        gathered(2)
        add_d(1, 2, True)
        placed(3)
        gathered(3)
        shared_e(1, 2)
        add_ef(1, 2, True, True, False)
        own.append(activate(1, 2))
        add_d(3, 1, True)
        wd_wait()
        project_df(1, 2)
        shared_e(3)
        add_ef(3, 1, True, True, False)
        own.append(activate(3))
        project_df(3)
        project_df(0)
        combine(1)
        combine(2)
        for i in range(3):
            copies.arrived(s_bz + i, f_zin.at[i])
        s_bup, s_bdown = copies.take(), copies.take()
        s_bup2, s_bdown2 = copies.take(), copies.take()
        for ky in (3, 2, 1, 0):
            f_sum[ky, z % 2] = total_of(f_part[0, ky], f_zin[2, ky])
            f_sum[ky, 1 - z % 2] = total_of(f_zin[0, ky], f_zin[1, ky])
            if ky == 3:
                own.append(copies.send(s_bup, f_sum.at[3, 0], f_up, y_up))
                own.append(copies.send(s_bdown, f_sum.at[3, 1], f_down, y_down))
        combine(3)
        combine(0)
        copies.arrived(s_bup, f_up)
        f_sum[2, 0] = total_of(f_sum[2, 0], f_up[...])
        own.append(copies.send(s_bup2, f_sum.at[2], f_up2, y_up))
        copies.arrived(s_bdown, f_down)
        f_sum[1, 1] = total_of(f_sum[1, 1], f_down[...])
        own.append(copies.send(s_bdown2, f_sum.at[1], f_down2, y_down))
        for i in range(3):
            copies.arrived(s_bdz + i, d_zin.at[i])
        value = total_of(d_group[0], d_zin[0], d_zin[1], d_zin[2])
        d_sum[...] = value.reshape(4, rows, WIDE)
        s_dy = copies.take(3)
        for i in range(3):
            own.append(copies.send(s_dy + i, d_sum.at[i + 1], d_yin.at[i], y_to[home[i]]))
        copies.arrived(s_bup2, f_up2)
        copies.arrived(s_bdown2, f_down2)
        f_sum[0] = total_of(f_sum[0], f_up2[...], f_down2[...])
        join_pairs(f_sum.at[0], f_back)
        s_x = copies.take(3)
        own += x_return(s_x, f_back, f_end)
        x_returned(s_x, f_end)
        value = hid[:, WIDE:] + weighted(f_end[...].reshape(slots, half - WIDE))
        last[:, WIDE:] = value.astype(BF16)
        value = hid[:, 0:WIDE] + d_sum[0].astype(F32)
        for i in range(3):
            copies.arrived(s_dy + i, d_yin.at[i])
            value = value + d_yin[i].astype(F32)
        last[:, 0:WIDE] = value.astype(BF16)
        pltpu.make_async_copy(last, o_ref.at[:, mine], load_sems.at[0]).start()
        own.append(copies.send(s_last, last, o_ref.at[:, mine], other))
        for copy in own:
            copy.wait_send()

    common = copies.used
    pl.when(c == 0)(core_zero)
    used_zero, copies.used = copies.used, common
    pl.when(c == 1)(core_one)
    assert max(used_zero, copies.used) <= SEMS

    copies.arrived(s_last, o_ref.at[:, theirs])
    pltpu.make_async_copy(last, o_ref.at[:, mine], load_sems.at[0]).wait()
    for copy in sent:
        copy.wait_send()


def on_device(
    queries,
    new_keys,
    new_values,
    fork_map,
    key_cache,
    value_cache,
    cache_lengths,
    residual,
    norm_gain,
    expert_ids,
    gate_weights,
    w_gate,
    w_up,
    w_down,
):
    rows, width = residual.shape
    half = width // 2
    narrow = half - WIDE
    hidden = w_gate.shape[2]
    prompts, cache_len, kv_width = key_cache.shape
    heads = kv_width // HD
    vmem = pl.BlockSpec(memory_space=VMEM)
    hbm = pl.BlockSpec(memory_space=pl.ANY)
    return pl.pallas_call(
        layer_kernel,
        out_shape=jax.ShapeDtypeStruct((rows, width), BF16),
        in_specs=[pl.BlockSpec(memory_space=pltpu.SMEM)] + [vmem] * 4 + [hbm] * 9,
        out_specs=hbm,
        scratch_shapes=[
            VMEM((rows, half), BF16),
            VMEM((rows, kv_width), BF16),
            VMEM((rows, kv_width), BF16),
            VMEM((heads, prompts, cache_len, HD), BF16),
            VMEM((heads, prompts, cache_len, HD), BF16),
            VMEM((rows, half), BF16),
            VMEM((width, hidden), BF16),
            VMEM((width, hidden), BF16),
            VMEM((2 * hidden, half), BF16),
            VMEM((2, rows, HD), F32),
            VMEM((rows, half), F32),
            VMEM((512, hidden), F32),
            VMEM((512, hidden), F32),
            VMEM((2, 512, hidden), BF16),
            VMEM((rows, half), BF16),
            VMEM((4, 16, half), BF16),
            VMEM((4, 16, half), BF16),
            VMEM((2, 32, half), BF16),
            VMEM((4, 4, 32, half), BF16),
            VMEM((4, 4, 32, half), BF16),
            VMEM((4, 16, half), BF16),
            VMEM((4, 16, half), BF16),
            VMEM((4, 32, half), BF16),
            VMEM((4, 32, half), BF16),
            VMEM((3, 32, half), BF16),
            VMEM((2, 32, half), BF16),
            VMEM((4, 16, half), BF16),
            VMEM((4, 16, half), BF16),
            VMEM((4, 16, narrow), BF16),
            VMEM((4, 16, narrow), BF16),
            VMEM((2, 32, narrow), BF16),
            VMEM((3, 2, 32, narrow), BF16),
            VMEM((4, 4, 32, narrow), BF16),
            VMEM((4, 4, 32, narrow), BF16),
            VMEM((3, 4, 32, narrow), BF16),
            VMEM((4, 2, 32, narrow), BF16),
            VMEM((32, narrow), BF16),
            VMEM((32, narrow), BF16),
            VMEM((2, 32, narrow), BF16),
            VMEM((2, 32, narrow), BF16),
            VMEM((4, 16, narrow), BF16),
            VMEM((4, 16, narrow), BF16),
            VMEM((4, 4, rows, WIDE + HD), BF16),
            VMEM((4, 2, 4 * rows, HD), BF16),
            VMEM((4, 4, 32, WIDE), BF16),
            VMEM((4, 4, 32, WIDE), BF16),
            VMEM((4, 4, 32, WIDE), BF16),
            VMEM((4, 4, 32, WIDE), BF16),
            VMEM((4, 4 * rows, WIDE), BF16),
            VMEM((3, 4 * rows, WIDE), BF16),
            VMEM((4, rows, WIDE), BF16),
            VMEM((3, rows, WIDE), BF16),
            pltpu.SemaphoreType.DMA((SEMS,)),
            pltpu.SemaphoreType.DMA((SEMS,)),
            pltpu.SemaphoreType.DMA((7 + 2 * heads,)),
            pltpu.SemaphoreType.REGULAR,
        ],
        compiler_params=pltpu.CompilerParams(
            collective_id=0, has_side_effects=True, vmem_limit_bytes=60 * 2**20
        ),
    )(
        cache_lengths,
        fork_map.reshape(1, rows),
        norm_gain.reshape(width // HD, HD),
        expert_ids.T,
        gate_weights.T,
        queries,
        new_keys,
        new_values,
        key_cache,
        value_cache,
        residual,
        w_gate[0],
        w_up[0],
        w_down[0],
    )


def solution(mesh):
    in_specs = (
        P(("grp", "shard"), "pool"),
        P(("grp", "shard"), "pool"),
        P(("grp", "shard"), "pool"),
        P(("grp", "shard")),
        P(("grp", "shard"), None, "pool"),
        P(("grp", "shard"), None, "pool"),
        P(("grp", "shard")),
        P(("grp", "shard"), None),
        P(),
        P(("grp", "shard"), None),
        P(("grp", "shard"), None),
        P("grp", None, ("pool", "shard")),
        P("grp", None, ("pool", "shard")),
        P("grp", ("pool", "shard"), None),
    )
    out_specs = P(("grp", "shard"), None)
    return jax.shard_map(
        on_device, mesh=mesh, in_specs=in_specs, out_specs=out_specs, check_vma=False
    )
```
